256 devices in a mesh: band: 32 (over x_lo, z, core), grid: 8 (over x_hi, y).
Axes of the slice: x: 4 (x_hi: 2, x_lo: 2; x = x_hi * 2 + x_lo), y: 4, z: 8, core: 2. Of those that a mesh axis runs over, the one named last changes fastest.
Arguments:
- bands: float32 [64, 120, 14400], P('band', 'grid'), may hold values from -6 to 6
- occupations: float32 [64], P('band'), may hold values from 0.2 to 1
Outputs:
- exchange_term: float32 [64, 120, 14400], P('band', 'grid')
The draws below stay inside these ranges and needn't reach their ends.
All inputs are finite; a program needn't handle non-finite values.
Results may differ from the reference program's by a relative error of at most 0.02.
Values may be sent and summed in bfloat16 or wider, within the bound.
A program may use at most 64 MiB of HBM per device.

```python
import math
import jax
import jax.numpy as jnp
from jax import lax

NG = 120
BLOCK = 2
BANDS = 64
N_BAND = 32


def block_scale(rng, extent, cuts, least, top_value):
    factor_of = 1.0
    for axis_at, shards_of in cuts:
        steps = jax.random.uniform(jax.random.fold_in(jax.random.fold_in(rng, 6), axis_at), (shards_of,), jnp.float32, least / len(cuts), top_value / len(cuts))
        factor_of = factor_of * jnp.repeat(jnp.exp(steps), extent[axis_at] // shards_of).reshape((-1,) + (1,) * (len(extent) - 1 - axis_at))
    return factor_of


def noise(key, shape, spread, reach, shards=(), kind=jnp.bfloat16):
    values = spread * jax.random.normal(key, shape, jnp.float32)
    if shards:
        values = values * block_scale(key, shape, shards, -0.22, 0.18)
    return jnp.clip(values, -reach, reach).astype(kind)


def setup_inputs(seed: int = 0) -> dict:
    arg_keys = jax.random.split(jax.random.key(seed), 3)
    return {
        "bands": noise(arg_keys[0], (BANDS, NG, NG * NG), 1.0, 6.0, ((0, 32), (1, 8)), jnp.float32),
        "occupations": jnp.clip(0.2 + 0.8 * jax.random.uniform(arg_keys[1], (BANDS,), jnp.float32) ** block_scale(arg_keys[1], (BANDS,), ((0, 32),), -0.2, 0.2), 0.2, 1.0),
    }


COULOMB = 160.0

def cas_matrix(points):
    indices = jnp.arange(points, dtype=jnp.int32)
    product = indices[:, None] * indices[None, :] % points
    phases = product.astype(jnp.float32) * (2.0 * math.pi / points)
    return ((jnp.cos(phases) + jnp.sin(phases)) / math.sqrt(points)).astype(jnp.bfloat16)

def frequency(indices, points):
    folded = jnp.where(indices <= points // 2, indices, indices - points).astype(jnp.float32)
    return folded * folded

def coulomb(first_sq, second_sq, third_sq):
    squared = first_sq[:, None, None] + second_sq[None, :, None] + third_sq[None, None, :]
    return jnp.where(squared > 0.5, COULOMB / jnp.maximum(squared, 1.0), 0.0)

def apply_third(values, matrix):
    return jnp.einsum('pxyz,kz->pxyk', values.astype(jnp.float32), matrix.astype(jnp.float32))

def apply_second(values, matrix):
    return jnp.einsum('pxyz,ky->pxkz', values.astype(jnp.float32), matrix.astype(jnp.float32))

def apply_first(values, matrix):
    return jnp.einsum('pxyz,kx->pkyz', values.astype(jnp.float32), matrix.astype(jnp.float32))

def reference(bands, occupations):
    groups = N_BAND
    points = NG
    hartley = cas_matrix(points)
    squares_axis = frequency(jnp.arange(points, dtype=jnp.int32), points)
    kernel_full = coulomb(squares_axis, squares_axis, squares_axis)
    stacked = bands.reshape(groups, BLOCK, points, points, points)
    weights = occupations.reshape(groups, BLOCK)

    def one_round(index):
        own = stacked[index]
        before = (index - 1) % groups
        partner = stacked[before]
        own_occ = weights[index]
        partner_occ = weights[before]
        density = (own[:, None] * partner[None, :]).astype(jnp.bfloat16)
        density = density.reshape(BLOCK * BLOCK, points, points, points)
        spectrum = apply_third(density, hartley).astype(jnp.bfloat16)
        spectrum = apply_second(spectrum, hartley).astype(jnp.bfloat16)
        spectrum = apply_first(spectrum, hartley).astype(jnp.bfloat16)
        scaled = (spectrum.astype(jnp.float32) * kernel_full).astype(jnp.bfloat16)
        inverse = apply_first(scaled, hartley).astype(jnp.bfloat16)
        inverse = apply_second(inverse, hartley).astype(jnp.bfloat16)
        potential = apply_third(inverse, hartley)
        potential = potential.reshape(BLOCK, BLOCK, points, points, points)
        local_term = -lax.optimization_barrier(jnp.sum(potential * (partner_occ[None, :, None, None, None] * partner[None]), axis=1))
        partner_term = -lax.optimization_barrier(jnp.sum(potential * (own_occ[:, None, None, None, None] * own[:, None]), axis=0))
        return (local_term, partner_term)
    local_all, partner_all = lax.map(one_round, jnp.arange(groups, dtype=jnp.int32))
    total = local_all + jnp.roll(partner_all, -1, axis=0)
    return total.reshape(BLOCK * groups, points, points * points)
```

```python
import functools
import math

import jax
import jax.numpy as jnp
import ml_dtypes
import numpy as np
from jax import lax
from jax.experimental import pallas as pl
from jax.experimental.pallas import tpu as pltpu
from jax.sharding import PartitionSpec as P

COULOMB = 160.0
NG = 120
PAD = 128
GRID = 8
PLANES = 15
MEMBERS = 2
ROWS = 32
SURFACE = NG * NG
MESH = pl.DeviceIdType.MESH
BF = jnp.bfloat16
F32 = jnp.float32


def tables():
    n = np.arange(NG)
    angle = (n[:, None] * n[None, :] % NG).astype(np.float32) * np.float32(2.0 * math.pi / NG)
    h = (np.cos(angle) + np.sin(angle)) / np.float32(math.sqrt(NG))
    padded = np.zeros((PAD, PAD), np.float32)
    padded[:NG, :NG] = h
    second = np.zeros((GRID, MEMBERS, 16, MEMBERS, PAD), np.float32)
    for p in range(MEMBERS):
        second[:, p, :PLANES, p, :NG] = h.reshape(GRID, PLANES, NG)
    second = second.reshape(GRID * ROWS, MEMBERS * PAD)
    return (
        padded.astype(ml_dtypes.bfloat16),
        second.astype(ml_dtypes.bfloat16),
        np.ascontiguousarray(second.T).astype(ml_dtypes.bfloat16),
    )


def dot(a, b):
    return jnp.dot(a, b, preferred_element_type=F32)


def square(index):
    folded = jnp.where(index <= NG // 2, index, index - NG).astype(F32)
    return folded * folded


def kernel(bands, occ, h_ref, second_ref, second_t_ref, out,
           xin, rows32, own, part, occ_mine, occ_part, coul, send, got, wide, wide2,
           back_send, back, local, ret, ret_got,
           in_sem, sh_send, sh_recv, oc_send, oc_recv, f_send, f_recv, f_own,
           b_send, b_recv, b_own, r_send, r_recv):
    me_b = lax.axis_index("band")
    me = lax.axis_index("grid")
    groups = lax.axis_size("band")
    ahead = {"band": lax.rem(me_b + 1, groups)}
    behind = {"band": lax.rem(me_b + groups - 1, groups)}

    loads = [pltpu.make_async_copy(bands.at[i], xin.at[i], in_sem.at[i]) for i in range(MEMBERS)]
    for c in loads:
        c.start()

    barrier = pltpu.get_barrier_semaphore()
    for d in range(1, GRID):
        pl.semaphore_signal(barrier, inc=1, device_id={"grid": lax.rem(me + d, GRID)}, device_id_type=MESH)
    pl.semaphore_signal(barrier, inc=1, device_id=ahead, device_id_type=MESH)
    pl.semaphore_signal(barrier, inc=1, device_id=behind, device_id_type=MESH)

    lane = lax.broadcasted_iota(jnp.int32, (PLANES, PAD), 1)
    rows32[pl.ds(NG * 16, 8 * 16), :] = jnp.zeros((8 * 16, PAD), F32)
    wide[pl.ds(NG * ROWS, 8 * ROWS), :] = jnp.zeros((8 * ROWS, PAD), F32)
    for p in range(MEMBERS):
        wide2[pl.ds(p * 16 + 15, PAD, stride=ROWS), :] = jnp.zeros((PAD, PAD), F32)
    row = lax.broadcasted_iota(jnp.int32, (8, PAD), 0)
    occ_mine[...] = jnp.where(row == 0, occ[0], occ[1])

    shifts = []
    for i in range(MEMBERS):
        loads[i].wait()
        for r in range(NG):
            tile, off = divmod(NG * r, PAD)
            a = xin[i, :, tile * PAD:(tile + 1) * PAD]
            if off > PAD - NG:
                if (tile + 2) * PAD <= SURFACE:
                    b = xin[i, :, (tile + 1) * PAD:(tile + 2) * PAD]
                else:
                    rest = SURFACE - (tile + 1) * PAD
                    b = jnp.concatenate(
                        [xin[i, :, (tile + 1) * PAD:SURFACE], jnp.zeros((PLANES, PAD - rest), F32)], axis=1)
                a = jnp.where(lane >= off, a, b)
            if off:
                a = pltpu.roll(a, PAD - off, 1)
            rows32[pl.ds(r * 16, PLANES), :] = jnp.where(lane < NG, a, 0.0)

        def to_planes(x, _, i=i):
            own[i, x] = rows32[pl.ds(x, PAD, stride=16), :].astype(BF)
            return 0
        lax.fori_loop(0, PLANES, to_planes, 0, unroll=5)
        if i == 0:
            pl.semaphore_wait(barrier, GRID + 1)
            shift = pltpu.make_async_remote_copy(
                occ_mine, occ_part, oc_send, oc_recv, device_id=ahead, device_id_type=MESH)
            shift.start()
            shifts.append(shift)
        shift = pltpu.make_async_remote_copy(
            own.at[i], part.at[i], sh_send.at[i], sh_recv.at[i], device_id=ahead, device_id_type=MESH)
        shift.start()
        shifts.append(shift)

    kx = square(lax.broadcasted_iota(jnp.int32, (PAD, PAD), 0))
    kz = square(lax.broadcasted_iota(jnp.int32, (PAD, PAD), 1))
    plane_sq = kx + kz

    def fill(l, _):
        s = plane_sq + square(me * PLANES + l)
        coul[l] = jnp.where(s > 0.5, COULOMB / jnp.maximum(s, 1.0), 0.0)
        return 0
    lax.fori_loop(0, PLANES, fill, 0)

    sends = []
    for j in range(MEMBERS):
        shifts[1 + j].wait_recv()

        def forward(x, _, j=j):
            v = part[j, x]
            d = jnp.concatenate([own[0, x] * v, own[1, x] * v], axis=0)
            t = dot(d, h_ref[...]).astype(BF)
            send[j, x] = dot(second_ref[...], t).astype(BF)
            return 0
        lax.fori_loop(0, PLANES, forward, 0, unroll=3)

        mine = pltpu.make_async_copy(
            send.at[j, :, pl.ds(pl.multiple_of(me * ROWS, ROWS), ROWS)],
            got.at[j, pl.ds(me * PLANES, PLANES)], f_own.at[j])
        mine.start()
        chunk = [mine]
        for d in range(1, GRID):
            to = lax.rem(me + d, GRID)
            c = pltpu.make_async_remote_copy(
                send.at[j, :, pl.ds(pl.multiple_of(to * ROWS, ROWS), ROWS)],
                got.at[j, pl.ds(me * PLANES, PLANES)],
                f_send.at[j, d], f_recv.at[j, d], device_id={"grid": to}, device_id_type=MESH)
            c.start()
            chunk.append(c)
        sends.append(chunk)

    backs = []
    for j in range(MEMBERS):
        sends[j][0].wait()
        for c in sends[j][1:]:
            c.wait_recv()

        def widen(x, _, j=j):
            wide[pl.ds(pl.multiple_of(x * ROWS, ROWS), ROWS), :] = got[j, x].astype(F32)
            return 0
        lax.fori_loop(0, NG, widen, 0, unroll=8)

        def solve(l, _):
            r = jnp.concatenate(
                [wide[pl.ds(l, PAD, stride=ROWS), :], wide[pl.ds(16 + l, PAD, stride=ROWS), :]], axis=1)
            f = dot(h_ref[...], r.astype(BF))
            k = coul[l]
            f = (f * jnp.concatenate([k, k], axis=1)).astype(BF)
            g = dot(h_ref[...], f)
            wide2[pl.ds(l, PAD, stride=ROWS), :] = g[:, :PAD]
            wide2[pl.ds(16 + l, PAD, stride=ROWS), :] = g[:, PAD:]
            return 0
        lax.fori_loop(0, PLANES, solve, 0, unroll=3)

        def narrow(x, _, j=j):
            back_send[j, x] = wide2[pl.ds(pl.multiple_of(x * ROWS, ROWS), ROWS), :].astype(BF)
            return 0
        lax.fori_loop(0, NG, narrow, 0, unroll=8)

        mine = pltpu.make_async_copy(
            back_send.at[j, pl.ds(me * PLANES, PLANES)],
            back.at[j, :, pl.ds(pl.multiple_of(me * ROWS, ROWS), ROWS)], b_own.at[j])
        mine.start()
        chunk = [mine]
        for d in range(1, GRID):
            to = lax.rem(me + d, GRID)
            c = pltpu.make_async_remote_copy(
                back_send.at[j, pl.ds(to * PLANES, PLANES)],
                back.at[j, :, pl.ds(pl.multiple_of(me * ROWS, ROWS), ROWS)],
                b_send.at[j, d], b_recv.at[j, d], device_id={"grid": to}, device_id_type=MESH)
            c.start()
            chunk.append(c)
        backs.append(chunk)

    shifts[0].wait_recv()
    returns = []
    for j in range(MEMBERS):
        backs[j][0].wait()
        for c in backs[j][1:]:
            c.wait_recv()

        def inverse(x, _, j=j):
            u = dot(second_t_ref[...], back[j, x]).astype(BF)
            v = dot(u, h_ref[...])
            v0, v1 = v[:PAD], v[PAD:]
            w = part[j, x].astype(F32) * occ_part[pl.ds(j, 1), :]
            row0 = pl.ds(pl.multiple_of(x * PAD, PAD), PAD)
            row1 = pl.ds(pl.multiple_of((PLANES + x) * PAD, PAD), PAD)
            if j == 0:
                local[row0, :] = -(v0 * w)
                local[row1, :] = -(v1 * w)
            else:
                local[row0, :] -= v0 * w
                local[row1, :] -= v1 * w
            q = (v0 * (own[0, x].astype(F32) * occ_mine[pl.ds(0, 1), :])
                 + v1 * (own[1, x].astype(F32) * occ_mine[pl.ds(1, 1), :]))
            ret[j, x] = (-q).astype(BF)
            return 0
        lax.fori_loop(0, PLANES, inverse, 0, unroll=3)
        c = pltpu.make_async_remote_copy(
            ret.at[j], ret_got.at[j], r_send.at[j], r_recv.at[j], device_id=behind, device_id_type=MESH)
        c.start()
        returns.append(c)

    local[pl.ds(2 * PLANES * PAD, PAD), :] = jnp.zeros((PAD, PAD), F32)
    for i in range(MEMBERS):
        returns[i].wait_recv()

        def total(x, _, i=i):
            rows = pl.ds(pl.multiple_of((i * PLANES + x) * PAD, PAD), PAD)
            local[rows, :] += ret_got[i, x].astype(F32)
            return 0
        lax.fori_loop(0, PLANES, total, 0, unroll=3)

        rolled = []
        for r in range(NG):
            tile = -(-NG * r // PAD)
            first = PAD * tile - NG * r
            v = local[pl.ds(i * PLANES * PAD + r, 16, stride=PAD), :]
            rolled.append(pltpu.roll(v, PAD - first, 1) if first else v)
            if r % 16:
                t = tile - 1
                z0 = PAD * t - NG * (r - 1)
                full = jnp.where(lane < NG - z0, rolled[r - 1][:PLANES], rolled[r][:PLANES])
                out[i, :, t * PAD:(t + 1) * PAD] = full
        out[i, :, SURFACE - 64:] = rolled[NG - 1][:PLANES, :64]

    for c in shifts:
        c.wait_send()
    for chunk in sends + backs:
        for c in chunk[1:]:
            c.wait_send()
    for c in returns:
        c.wait_send()


def per_device(bands, occupations):
    h, second, second_t = (jnp.asarray(t) for t in tables())
    dma = pltpu.SemaphoreType.DMA
    vmem = pl.BlockSpec(memory_space=pltpu.VMEM)
    return pl.pallas_call(
        kernel,
        out_shape=jax.ShapeDtypeStruct(bands.shape, F32),
        in_specs=[pl.BlockSpec(memory_space=pl.ANY), pl.BlockSpec(memory_space=pltpu.SMEM), vmem, vmem, vmem],
        out_specs=vmem,
        scratch_shapes=[
            pltpu.VMEM((MEMBERS, PLANES, SURFACE), F32),
            pltpu.VMEM((PAD * 16, PAD), F32),
            pltpu.VMEM((MEMBERS, PLANES, PAD, PAD), BF),
            pltpu.VMEM((MEMBERS, PLANES, PAD, PAD), BF),
            pltpu.VMEM((8, PAD), F32),
            pltpu.VMEM((8, PAD), F32),
            pltpu.VMEM((PLANES, PAD, PAD), F32),
            pltpu.VMEM((MEMBERS, PLANES, GRID * ROWS, PAD), BF),
            pltpu.VMEM((MEMBERS, NG, ROWS, PAD), BF),
            pltpu.VMEM((PAD * ROWS, PAD), F32),
            pltpu.VMEM((PAD * ROWS, PAD), F32),
            pltpu.VMEM((MEMBERS, NG, ROWS, PAD), BF),
            pltpu.VMEM((MEMBERS, PLANES, GRID * ROWS, PAD), BF),
            pltpu.VMEM(((2 * PLANES + 1) * PAD, PAD), F32),
            pltpu.VMEM((MEMBERS, PLANES, PAD, PAD), BF),
            pltpu.VMEM((MEMBERS, PLANES, PAD, PAD), BF),
            dma((MEMBERS,)), dma((MEMBERS,)), dma((MEMBERS,)), dma, dma,
            dma((MEMBERS, GRID)), dma((MEMBERS, GRID)), dma((MEMBERS,)),
            dma((MEMBERS, GRID)), dma((MEMBERS, GRID)), dma((MEMBERS,)),
            dma((MEMBERS,)), dma((MEMBERS,)),
        ],
        compiler_params=pltpu.CompilerParams(
            collective_id=0, has_side_effects=True, vmem_limit_bytes=48 * 2**20),
    )(bands, occupations, h, second, second_t)


def solution(mesh):
    return jax.shard_map(
        per_device,
        mesh=mesh,
        in_specs=(P("band", "grid", None), P("band")),
        out_specs=P("band", "grid", None),
        check_vma=False,
    )
```

```python
import functools
import math

import jax
import jax.numpy as jnp
import ml_dtypes
import numpy as np
from jax import lax
from jax.experimental import pallas as pl
from jax.experimental.pallas import tpu as pltpu
from jax.sharding import PartitionSpec as P

COULOMB = 160.0
NG = 120
PAD = 128
GRID = 8
PLANES = 15
MEMBERS = 2
ROWS = 32
XG = 5
NQ = PLANES // XG
SURFACE = NG * NG
MESH = pl.DeviceIdType.MESH
BF = jnp.bfloat16
F32 = jnp.float32


def tables():
    n = np.arange(NG)
    angle = (n[:, None] * n[None, :] % NG).astype(np.float32) * np.float32(2.0 * math.pi / NG)
    h = (np.cos(angle) + np.sin(angle)) / np.float32(math.sqrt(NG))
    padded = np.zeros((PAD, PAD), np.float32)
    padded[:NG, :NG] = h
    second = np.zeros((GRID, MEMBERS, 16, MEMBERS, PAD), np.float32)
    for p in range(MEMBERS):
        second[:, p, :PLANES, p, :NG] = h.reshape(GRID, PLANES, NG)
    second = second.reshape(GRID * ROWS, MEMBERS * PAD)
    return (
        padded.astype(ml_dtypes.bfloat16),
        second.astype(ml_dtypes.bfloat16),
        np.ascontiguousarray(second.T).astype(ml_dtypes.bfloat16),
    )


def dot(a, b):
    return jnp.dot(a, b, preferred_element_type=F32)


def square(index):
    folded = jnp.where(index <= NG // 2, index, index - NG).astype(F32)
    return folded * folded


def kernel(bands, occ, h_hbm, second_hbm, second_t_hbm, out,
           xin, rows32, own, part, occ_mine, occ_part, coul, send, got, wide, wide2,
           back_send, back, local, ret, ret_got, xout, h_ref, second_ref, second_t_ref,
           in_sem, c_sem, out_sem, sh_send, sh_recv, oc_send, oc_recv, f_send, f_recv, f_own,
           b_send, b_recv, b_own, r_send, r_recv):
    me_b = lax.axis_index("band")
    me = lax.axis_index("grid")
    groups = lax.axis_size("band")
    ahead = {"band": lax.rem(me_b + 1, groups)}
    behind = {"band": lax.rem(me_b + groups - 1, groups)}

    def span(q):
        return pl.ds(q * XG, XG)

    loads = [pltpu.make_async_copy(bands.at[span(q)], xin.at[span(q)], in_sem.at[q]) for q in range(NQ)]
    consts = [
        pltpu.make_async_copy(src, dst, c_sem.at[n])
        for n, (src, dst) in enumerate(
            ((h_hbm, h_ref), (second_hbm, second_ref), (second_t_hbm, second_t_ref)))
    ]
    for c in loads + consts:
        c.start()

    barrier = pltpu.get_barrier_semaphore()
    for d in range(1, GRID):
        pl.semaphore_signal(barrier, inc=1, device_id={"grid": lax.rem(me + d, GRID)}, device_id_type=MESH)
    pl.semaphore_signal(barrier, inc=1, device_id=ahead, device_id_type=MESH)
    pl.semaphore_signal(barrier, inc=1, device_id=behind, device_id_type=MESH)

    lane = lax.broadcasted_iota(jnp.int32, (MEMBERS, PAD), 1)
    rows32[pl.ds(NG * MEMBERS, 8 * MEMBERS), :] = jnp.zeros((8 * MEMBERS, PAD), F32)
    wide[pl.ds(NG * ROWS, 8 * ROWS), :] = jnp.zeros((8 * ROWS, PAD), F32)
    for p in range(MEMBERS):
        wide2[pl.ds(p * 16 + 15, PAD, stride=ROWS), :] = jnp.zeros((PAD, PAD), F32)
    row = lax.broadcasted_iota(jnp.int32, (8, PAD), 0)
    occ_mine[...] = jnp.where(row == 0, occ[0], occ[1])

    def unpack(x, _):
        tiles = {}

        def tile_of(t):
            if t not in tiles:
                if (t + 1) * PAD <= SURFACE:
                    tiles[t] = xin[x, :, t * PAD:(t + 1) * PAD]
                else:
                    half = xin[x, :, t * PAD:SURFACE]
                    tiles[t] = jnp.concatenate([half, jnp.zeros_like(half)], axis=1)
            return tiles[t]

        for r in range(NG):
            tile, off = divmod(NG * r, PAD)
            a = tile_of(tile)
            if off > PAD - NG:
                a = jnp.where(lane >= off, a, tile_of(tile + 1))
            if off:
                a = pltpu.roll(a, PAD - off, 1)
            rows32[pl.ds(r * MEMBERS, MEMBERS), :] = jnp.where(lane < NG, a, 0.0)
        for i in range(MEMBERS):
            own[i, x] = rows32[pl.ds(i, PAD, stride=MEMBERS), :].astype(BF)
        return 0

    def shift_of(j, q):
        return pltpu.make_async_remote_copy(
            own.at[j, span(q)], part.at[j, span(q)], sh_send.at[j, q], sh_recv.at[j, q],
            device_id=ahead, device_id_type=MESH)

    shifts = [[shift_of(j, q) for q in range(NQ)] for j in range(MEMBERS)]
    occ_shift = pltpu.make_async_remote_copy(
        occ_mine, occ_part, oc_send, oc_recv, device_id=ahead, device_id_type=MESH)
    for q in range(NQ):
        loads[q].wait()
        lax.fori_loop(q * XG, (q + 1) * XG, unpack, 0)
        if q == 0:
            pl.semaphore_wait(barrier, GRID + 1)
        shifts[0][q].start()
    for q in range(NQ):
        shifts[1][q].start()
    occ_shift.start()

    kx = square(lax.broadcasted_iota(jnp.int32, (PAD, PAD), 0))
    kz = square(lax.broadcasted_iota(jnp.int32, (PAD, PAD), 1))
    plane_sq = kx + kz

    def fill(l, _):
        s = plane_sq + square(me * PLANES + l)
        coul[l] = jnp.where(s > 0.5, COULOMB / jnp.maximum(s, 1.0), 0.0)
        return 0
    lax.fori_loop(0, PLANES, fill, 0)
    for c in consts:
        c.wait()

    mine_rows = pl.ds(pl.multiple_of(me * ROWS, ROWS), ROWS)
    sends = []
    for j in range(MEMBERS):
        for q in range(NQ):
            shifts[j][q].wait_recv()

            def forward(x, _, j=j):
                v = part[j, x]
                d = jnp.concatenate([own[0, x] * v, own[1, x] * v], axis=0)
                t = dot(d, h_ref[...]).astype(BF)
                send[j, x] = dot(second_ref[...], t).astype(BF)
                return 0
            lax.fori_loop(q * XG, (q + 1) * XG, forward, 0, unroll=XG)

            mine = pltpu.make_async_copy(
                send.at[j, span(q), mine_rows],
                got.at[j, pl.ds(me * PLANES + q * XG, XG)], f_own.at[j, q])
            mine.start()
            chunk = [mine]
            for d in range(1, GRID):
                to = lax.rem(me + d, GRID)
                c = pltpu.make_async_remote_copy(
                    send.at[j, span(q), pl.ds(pl.multiple_of(to * ROWS, ROWS), ROWS)],
                    got.at[j, pl.ds(me * PLANES + q * XG, XG)],
                    f_send.at[j, q, d], f_recv.at[j, q, d], device_id={"grid": to}, device_id_type=MESH)
                c.start()
                chunk.append(c)
            sends.append(chunk)

    backs = []
    for j in range(MEMBERS):
        for q in range(NQ):
            sends[j * NQ + q][0].wait()
            for c in sends[j * NQ + q][1:]:
                c.wait_recv()

        def widen(x, _, j=j):
            wide[pl.ds(pl.multiple_of(x * ROWS, ROWS), ROWS), :] = got[j, x].astype(F32)
            return 0
        lax.fori_loop(0, NG, widen, 0, unroll=8)

        def solve(l, _):
            r = jnp.concatenate(
                [wide[pl.ds(l, PAD, stride=ROWS), :], wide[pl.ds(16 + l, PAD, stride=ROWS), :]], axis=1)
            f = dot(h_ref[...], r.astype(BF))
            k = coul[l]
            f = (f * jnp.concatenate([k, k], axis=1)).astype(BF)
            g = dot(h_ref[...], f)
            wide2[pl.ds(l, PAD, stride=ROWS), :] = g[:, :PAD]
            wide2[pl.ds(16 + l, PAD, stride=ROWS), :] = g[:, PAD:]
            return 0
        lax.fori_loop(0, PLANES, solve, 0, unroll=5)

        for q in range(NQ):
            def narrow(g, _, j=j, q=q):
                for x in range(XG):
                    at = g * PLANES + q * XG + x
                    back_send[j, at] = wide2[pl.ds(pl.multiple_of(at * ROWS, ROWS), ROWS), :].astype(BF)
                return 0
            lax.fori_loop(0, GRID, narrow, 0, unroll=2)

            mine = pltpu.make_async_copy(
                back_send.at[j, pl.ds(me * PLANES + q * XG, XG)],
                back.at[j, span(q), mine_rows], b_own.at[j, q])
            mine.start()
            chunk = [mine]
            for d in range(1, GRID):
                to = lax.rem(me + d, GRID)
                c = pltpu.make_async_remote_copy(
                    back_send.at[j, pl.ds(to * PLANES + q * XG, XG)],
                    back.at[j, span(q), mine_rows],
                    b_send.at[j, q, d], b_recv.at[j, q, d], device_id={"grid": to}, device_id_type=MESH)
                c.start()
                chunk.append(c)
            backs.append(chunk)

    occ_shift.wait_recv()
    returns = []
    for j in range(MEMBERS):
        for q in range(NQ):
            backs[j * NQ + q][0].wait()
            for c in backs[j * NQ + q][1:]:
                c.wait_recv()

            def inverse(x, _, j=j):
                u = dot(second_t_ref[...], back[j, x]).astype(BF)
                v = dot(u, h_ref[...])
                v0, v1 = v[:PAD], v[PAD:]
                w = part[j, x].astype(F32) * occ_part[pl.ds(j, 1), :]
                if j == 0:
                    local[0, x] = -(v0 * w)
                    local[1, x] = -(v1 * w)
                else:
                    local[0, x] -= v0 * w
                    local[1, x] -= v1 * w
                s = (v0 * (own[0, x].astype(F32) * occ_mine[pl.ds(0, 1), :])
                     + v1 * (own[1, x].astype(F32) * occ_mine[pl.ds(1, 1), :]))
                ret[j, x] = (-s).astype(BF)
                return 0
            lax.fori_loop(q * XG, (q + 1) * XG, inverse, 0, unroll=XG)
            c = pltpu.make_async_remote_copy(
                ret.at[j, span(q)], ret_got.at[j, span(q)], r_send.at[j, q], r_recv.at[j, q],
                device_id=behind, device_id_type=MESH)
            c.start()
            returns.append(c)

    def pack(x, _):
        for i in range(MEMBERS):
            rows32[pl.ds(i, PAD, stride=MEMBERS), :] = local[i, x] + ret_got[i, x].astype(F32)
        before = None
        for r in range(NG):
            tile = -(-NG * r // PAD)
            first = PAD * tile - NG * r
            v = rows32[pl.ds(r * MEMBERS, MEMBERS), :]
            if first:
                v = pltpu.roll(v, PAD - first, 1)
            if r % 16:
                t = tile - 1
                z0 = PAD * t - NG * (r - 1)
                xout[x, :, t * PAD:(t + 1) * PAD] = jnp.where(lane < NG - z0, before, v)
            before = v
        xout[x, :, SURFACE - 64:] = before[:, :64]
        return 0

    stores = []
    for q in range(NQ):
        for j in range(MEMBERS):
            returns[j * NQ + q].wait_recv()
        lax.fori_loop(q * XG, (q + 1) * XG, pack, 0)
        c = pltpu.make_async_copy(xout.at[span(q)], out.at[span(q)], out_sem.at[q])
        c.start()
        stores.append(c)

    for c in stores:
        c.wait()
    for c in shifts[0] + shifts[1] + [occ_shift] + returns:
        c.wait_send()
    for chunk in sends + backs:
        for c in chunk[1:]:
            c.wait_send()


def per_device(bands, occupations):
    h, second, second_t = (jnp.asarray(t) for t in tables())
    dma = pltpu.SemaphoreType.DMA
    hbm = pl.BlockSpec(memory_space=pl.ANY)
    planes_first = bands.transpose(1, 0, 2)
    total = pl.pallas_call(
        kernel,
        out_shape=jax.ShapeDtypeStruct(planes_first.shape, F32),
        in_specs=[hbm, pl.BlockSpec(memory_space=pltpu.SMEM), hbm, hbm, hbm],
        out_specs=hbm,
        scratch_shapes=[
            pltpu.VMEM((PLANES, MEMBERS, SURFACE), F32),
            pltpu.VMEM((PAD * MEMBERS, PAD), F32),
            pltpu.VMEM((MEMBERS, PLANES, PAD, PAD), BF),
            pltpu.VMEM((MEMBERS, PLANES, PAD, PAD), BF),
            pltpu.VMEM((8, PAD), F32),
            pltpu.VMEM((8, PAD), F32),
            pltpu.VMEM((PLANES, PAD, PAD), F32),
            pltpu.VMEM((MEMBERS, PLANES, GRID * ROWS, PAD), BF),
            pltpu.VMEM((MEMBERS, NG, ROWS, PAD), BF),
            pltpu.VMEM((PAD * ROWS, PAD), F32),
            pltpu.VMEM((PAD * ROWS, PAD), F32),
            pltpu.VMEM((MEMBERS, NG, ROWS, PAD), BF),
            pltpu.VMEM((MEMBERS, PLANES, GRID * ROWS, PAD), BF),
            pltpu.VMEM((MEMBERS, PLANES, PAD, PAD), F32),
            pltpu.VMEM((MEMBERS, PLANES, PAD, PAD), BF),
            pltpu.VMEM((MEMBERS, PLANES, PAD, PAD), BF),
            pltpu.VMEM((PLANES, MEMBERS, SURFACE), F32),
            pltpu.VMEM(h.shape, BF),
            pltpu.VMEM(second.shape, BF),
            pltpu.VMEM(second_t.shape, BF),
            dma((NQ,)), dma((3,)), dma((NQ,)),
            dma((MEMBERS, NQ)), dma((MEMBERS, NQ)), dma, dma,
            dma((MEMBERS, NQ, GRID)), dma((MEMBERS, NQ, GRID)), dma((MEMBERS, NQ)),
            dma((MEMBERS, NQ, GRID)), dma((MEMBERS, NQ, GRID)), dma((MEMBERS, NQ)),
            dma((MEMBERS, NQ)), dma((MEMBERS, NQ)),
        ],
        compiler_params=pltpu.CompilerParams(
            collective_id=0, has_side_effects=True, vmem_limit_bytes=58 * 2**20),
    )(planes_first, occupations, h, second, second_t)
    return total.transpose(1, 0, 2)


def solution(mesh):
    return jax.shard_map(
        per_device,
        mesh=mesh,
        in_specs=(P("band", "grid", None), P("band")),
        out_specs=P("band", "grid", None),
        check_vma=False,
    )
```

```python
import functools
import math

import jax
import jax.numpy as jnp
import ml_dtypes
import numpy as np
from jax import lax
from jax.experimental import pallas as pl
from jax.experimental.pallas import tpu as pltpu
from jax.sharding import PartitionSpec as P

COULOMB = 160.0
NG = 120
PAD = 128
GRID = 8
PLANES = 15
MEMBERS = 2
ROWS = 32
TILE = 16
OUT_GROUPS = ((0, 5), (5, 5), (10, 5))
BACK_GROUPS = ((0, 5), (5, 5), (10, 5))
NQ = len(OUT_GROUPS)
RELAY_Z = {1: 6, 2: 5}
RELAY_PLANES = max(OUT_GROUPS[q][1] for q in RELAY_Z)
SURFACE = NG * NG
MESH = pl.DeviceIdType.MESH
BF = jnp.bfloat16
F32 = jnp.float32


def tables():
    n = np.arange(NG)
    angle = (n[:, None] * n[None, :] % NG).astype(np.float32) * np.float32(2.0 * math.pi / NG)
    h = (np.cos(angle) + np.sin(angle)) / np.float32(math.sqrt(NG))
    padded = np.zeros((PAD, PAD), np.float32)
    padded[:NG, :NG] = h
    second = np.zeros((GRID * ROWS, MEMBERS, PAD), np.float32)
    for p in range(MEMBERS):
        second[p * NG:(p + 1) * NG, p, :NG] = h
    second = second.reshape(GRID * ROWS, MEMBERS * PAD)
    return (
        padded.astype(ml_dtypes.bfloat16),
        second.astype(ml_dtypes.bfloat16),
        np.ascontiguousarray(second.T).astype(ml_dtypes.bfloat16),
    )


def dot(a, b):
    return jnp.dot(a, b, preferred_element_type=F32)


def square(index):
    folded = jnp.where(index <= NG // 2, index, index - NG).astype(F32)
    return folded * folded


def kernel(bands, occ, h_hbm, second_hbm, second_t_hbm, out,
           xin, rows32, own, part, occ_mine, occ_part, coul, send, got, wide, wide2,
           back_send, back, local, ret, ret_got, xout, h_ref, second_ref, second_t_ref, relayed,
           in_sem, c_sem, out_sem, sh_send, sh_recv, oc_send, oc_recv, f_send, f_recv, f_own,
           b_send, b_recv, b_own, r_send, r_recv, re_send, re_recv):
    me_b = lax.axis_index("band")
    me = lax.axis_index("grid")
    groups = lax.axis_size("band")
    core = lax.rem(me_b, 2)
    ahead = {"band": lax.rem(me_b + 1, groups)}
    behind = {"band": lax.rem(me_b + groups - 1, groups)}

    side = groups // 2
    column = me_b // side
    place = lax.rem(me_b, side)
    first = place == 0
    last = place == side - 1
    other = (1 - column) * side

    def remote(src, dst, send_sem, recv_sem, to):
        return pltpu.make_async_remote_copy(
            src, dst, send_sem, recv_sem, device_id=to, device_id_type=MESH)

    def out_span(q):
        return pl.ds(*OUT_GROUPS[q])

    def back_span(q):
        return pl.ds(*BACK_GROUPS[q])

    loads = [
        pltpu.make_async_copy(bands.at[out_span(q)], xin.at[out_span(q)], in_sem.at[q]) for q in range(NQ)]
    consts = [
        pltpu.make_async_copy(src, dst, c_sem.at[n])
        for n, (src, dst) in enumerate(
            ((h_hbm, h_ref), (second_hbm, second_ref), (second_t_hbm, second_t_ref)))
    ]
    for c in loads + consts:
        c.start()

    def greet(to):
        pl.semaphore_signal(barrier, inc=1, device_id=to, device_id_type=MESH)

    barrier = pltpu.get_barrier_semaphore()
    for d in range(1, GRID):
        greet({"grid": lax.rem(me + d, GRID)})
    greet(ahead)
    greet(behind)
    greetings = GRID + 1 + jnp.where(last, len(RELAY_Z), 0)
    for z in RELAY_Z.values():
        @pl.when(place == 2 * z + 1)
        def _():
            greet({"band": other + side - 1})

        @pl.when(first)
        def _(z=z):
            greet({"band": column * side + 2 * z + 1})
        greetings += (place == 2 * z + 1).astype(jnp.int32)

    lane = lax.broadcasted_iota(jnp.int32, (MEMBERS, PAD), 1)
    rows32[pl.ds(NG * MEMBERS, 8 * MEMBERS), :] = jnp.zeros((8 * MEMBERS, PAD), F32)
    wide[pl.ds(NG * ROWS, 8 * ROWS), :] = jnp.zeros((8 * ROWS, PAD), F32)
    row = lax.broadcasted_iota(jnp.int32, (8, PAD), 0)
    occ_mine[...] = jnp.where(row == 0, occ[0], occ[1])

    def unpack(x, _):
        tiles = {}

        def tile_of(t):
            if t not in tiles:
                if (t + 1) * PAD <= SURFACE:
                    tiles[t] = xin[x, :, t * PAD:(t + 1) * PAD]
                else:
                    half = xin[x, :, t * PAD:SURFACE]
                    tiles[t] = jnp.concatenate([half, jnp.zeros_like(half)], axis=1)
            return tiles[t]

        for r in range(NG):
            tile, off = divmod(NG * r, PAD)
            a = tile_of(tile)
            if off > PAD - NG:
                a = jnp.where(lane >= off, a, tile_of(tile + 1))
            if off:
                a = pltpu.roll(a, PAD - off, 1)
            rows32[pl.ds(r * MEMBERS, MEMBERS), :] = jnp.where(lane < NG, a, 0.0)
        for i in range(MEMBERS):
            own[i, x] = rows32[pl.ds(i, PAD, stride=MEMBERS), :].astype(BF)
        return 0

    shifts = [[
        remote(own.at[j, out_span(q)], part.at[j, out_span(q)], sh_send.at[j, q], sh_recv.at[j, q], ahead)
        for q in range(NQ)] for j in range(MEMBERS)]

    def relay_room(j, q):
        return relayed.at[j, pl.ds(0, OUT_GROUPS[q][1])]

    def start_shift(j, q):
        if q not in RELAY_Z:
            shifts[j][q].start()
            return

        @pl.when(last)
        def _():
            remote(own.at[j, out_span(q)], relay_room(j, q), sh_send.at[j, q], re_recv.at[j],
                   {"band": other + 2 * RELAY_Z[q] + 1}).start()

        @pl.when(jnp.logical_not(last))
        def _():
            shifts[j][q].start()

    def handed_on(j, q):
        return remote(relay_room(j, q), part.at[j, out_span(q)], re_send.at[j], sh_recv.at[j, q],
                      {"band": column * side})

    def hand_on(j):
        for q, z in RELAY_Z.items():
            @pl.when(place == 2 * z + 1)
            def _(q=q):
                remote(relay_room(j, q), relay_room(j, q), re_send.at[j], re_recv.at[j], ahead).wait_recv()
                handed_on(j, q).start()

    occ_shift = remote(occ_mine, occ_part, oc_send, oc_recv, ahead)
    for q in range(NQ):
        loads[q].wait()
        lax.fori_loop(OUT_GROUPS[q][0], sum(OUT_GROUPS[q]), unpack, 0)
        if q == 0:
            pl.semaphore_wait(barrier, greetings)
        start_shift(0, q)
    for q in range(NQ):
        start_shift(1, q)
    occ_shift.start()

    lights = [lax.rem(core + j, 2) * (GRID // 2) + 2 * j + core for j in range(MEMBERS)]

    def row_of(j, g):
        return pl.multiple_of(lax.rem(g + 2 * GRID - 1 - lights[j], GRID) * ROWS, ROWS)

    def by_light(is_light, action):
        pl.when(is_light)(functools.partial(action, TILE))
        pl.when(jnp.logical_not(is_light))(functools.partial(action, ROWS))

    kx = square(lax.broadcasted_iota(jnp.int32, (PAD, PAD), 0))
    kz = square(lax.broadcasted_iota(jnp.int32, (PAD, PAD), 1))
    plane_sq = kx + kz
    for j in range(MEMBERS):
        start = row_of(j, me)

        def fill(l, _, j=j, start=start):
            s = plane_sq + square(lax.rem(start + l, NG))
            coul[j, l] = jnp.where(s > 0.5, COULOMB / jnp.maximum(s, 1.0), 0.0)
            return 0
        lax.fori_loop(0, ROWS, fill, 0)
    for j in range(MEMBERS):
        back[j, :, pl.ds(MEMBERS * NG, TILE)] = jnp.zeros((PLANES, TILE, PAD), BF)
    for c in consts:
        c.wait()
    hand_on(0)

    def taken(sem, planes, rows):
        view = send.at[0, pl.ds(0, planes), pl.ds(0, rows)]
        remote(view, view, sem, sem, ahead).wait_recv()

    most, full = (GRID - 2) * ROWS + TILE, (GRID - 1) * ROWS

    def out_sent(j, q):
        @pl.when(me == lights[j])
        def _():
            taken(f_send.at[j, q], OUT_GROUPS[q][1], full)

        @pl.when(me != lights[j])
        def _():
            taken(f_send.at[j, q], OUT_GROUPS[q][1], most)

    def back_sent(j, q):
        by_light(me == lights[j], lambda n: taken(b_send.at[j, q], BACK_GROUPS[q][1], (GRID - 1) * n))

    f_mine, b_mine = {}, {}
    for j in range(MEMBERS):
        for q in range(NQ):
            shifts[j][q].wait_recv()

            def forward(x, _, j=j):
                v = part[j, x]
                d = jnp.concatenate([own[0, x] * v, own[1, x] * v], axis=0)
                t = dot(d, h_ref[...]).astype(BF)
                send[j, x] = dot(second_ref[...], t).astype(BF)
                return 0
            lax.fori_loop(OUT_GROUPS[q][0], sum(OUT_GROUPS[q]), forward, 0, unroll=OUT_GROUPS[q][1])
            if j:
                out_sent(0, q)

            there = pl.ds(me * PLANES + OUT_GROUPS[q][0], OUT_GROUPS[q][1])
            f_mine[j, q] = pltpu.make_async_copy(
                send.at[j, out_span(q), pl.ds(row_of(j, me), ROWS)], got.at[j, there], f_own.at[j, q])
            f_mine[j, q].start()
            for d in range(1, GRID):
                to = lax.rem(me + d, GRID)

                def go(n, j=j, q=q, to=to, there=there):
                    remote(send.at[j, out_span(q), pl.ds(row_of(j, to), n)], got.at[j, there, pl.ds(0, n)],
                           f_send.at[j, q], f_recv.at[j, q], {"grid": to}).start()
                by_light(to == lights[j], go)
            if j == 0 and q == NQ - 1:
                hand_on(1)

    for j in range(MEMBERS):
        for q in range(NQ):
            f_mine[j, q].wait()
            by_light(me == lights[j],
                     lambda n, j=j, q=q: taken(f_recv.at[j, q], OUT_GROUPS[q][1], (GRID - 1) * n))

        def widen(x, _, j=j):
            wide[pl.ds(pl.multiple_of(x * ROWS, ROWS), ROWS), :] = got[j, x].astype(F32)
            return 0
        lax.fori_loop(0, NG, widen, 0, unroll=8)

        def solve(l, _, j=j):
            r = jnp.concatenate(
                [wide[pl.ds(l, PAD, stride=ROWS), :], wide[pl.ds(TILE + l, PAD, stride=ROWS), :]], axis=1)
            f = dot(h_ref[...], r.astype(BF))
            f = (f * jnp.concatenate([coul[j, l], coul[j, TILE + l]], axis=1)).astype(BF)
            g = dot(h_ref[...], f)
            wide2[pl.ds(l, PAD, stride=ROWS), :] = g[:, :PAD]
            wide2[pl.ds(TILE + l, PAD, stride=ROWS), :] = g[:, PAD:]
            return 0
        lax.fori_loop(0, TILE, solve, 0, unroll=4)

        for q in range(NQ):
            begin, planes = BACK_GROUPS[q]

            def narrow(g, _, j=j, begin=begin, planes=planes):
                for x in range(planes):
                    at = g * PLANES + begin + x
                    back_send[j, at] = wide2[pl.ds(pl.multiple_of(at * ROWS, ROWS), ROWS), :].astype(BF)
                return 0
            lax.fori_loop(0, GRID, narrow, 0, unroll=2)
            if j:
                back_sent(0, q)

            def go(n, j=j, q=q, begin=begin, planes=planes):
                here = back.at[j, back_span(q), pl.ds(row_of(j, me), n)]
                pltpu.make_async_copy(
                    back_send.at[j, pl.ds(me * PLANES + begin, planes), pl.ds(0, n)], here, b_own.at[j, q]).start()
                for d in range(1, GRID):
                    to = lax.rem(me + d, GRID)
                    remote(back_send.at[j, pl.ds(to * PLANES + begin, planes), pl.ds(0, n)], here,
                           b_send.at[j, q], b_recv.at[j, q], {"grid": to}).start()
            by_light(me == lights[j], go)

    def came_back(j, q):
        begin, planes = BACK_GROUPS[q]

        def wait(n):
            view = back_send.at[j, pl.ds(me * PLANES + begin, planes), pl.ds(0, n)]
            pltpu.make_async_copy(view, back.at[j, back_span(q), pl.ds(row_of(j, me), n)], b_own.at[j, q]).wait()
            taken(b_recv.at[j, q], planes, full if n == TILE else most)
        by_light(me == lights[j], wait)

    occ_shift.wait_recv()
    returns = [[
        remote(ret.at[j, back_span(q)], ret_got.at[j, back_span(q)], r_send.at[j, q], r_recv.at[j, q], behind)
        for q in range(NQ)] for j in range(MEMBERS)]
    for j in range(MEMBERS):
        for q in range(NQ):
            came_back(j, q)

            def inverse(x, _, j=j):
                u = dot(second_t_ref[...], back[j, x]).astype(BF)
                v = dot(u, h_ref[...])
                v0, v1 = v[:PAD], v[PAD:]
                w = part[j, x].astype(F32) * occ_part[pl.ds(j, 1), :]
                if j == 0:
                    local[0, x] = -(v0 * w)
                    local[1, x] = -(v1 * w)
                else:
                    local[0, x] -= v0 * w
                    local[1, x] -= v1 * w
                s = (v0 * (own[0, x].astype(F32) * occ_mine[pl.ds(0, 1), :])
                     + v1 * (own[1, x].astype(F32) * occ_mine[pl.ds(1, 1), :]))
                ret[j, x] = (-s).astype(BF)
                return 0
            lax.fori_loop(BACK_GROUPS[q][0], sum(BACK_GROUPS[q]), inverse, 0, unroll=BACK_GROUPS[q][1])
            returns[j][q].start()

    def pack(x, _):
        for i in range(MEMBERS):
            rows32[pl.ds(i, PAD, stride=MEMBERS), :] = local[i, x] + ret_got[i, x].astype(F32)
        before = None
        for r in range(NG):
            tile = -(-NG * r // PAD)
            begin = PAD * tile - NG * r
            v = rows32[pl.ds(r * MEMBERS, MEMBERS), :]
            if begin:
                v = pltpu.roll(v, PAD - begin, 1)
            if r % 16:
                t = tile - 1
                z0 = PAD * t - NG * (r - 1)
                xout[x, :, t * PAD:(t + 1) * PAD] = jnp.where(lane < NG - z0, before, v)
            before = v
        xout[x, :, SURFACE - 64:] = before[:, :64]
        return 0

    stores = []
    for q in range(NQ):
        for j in range(MEMBERS):
            returns[j][q].wait_recv()
        lax.fori_loop(BACK_GROUPS[q][0], sum(BACK_GROUPS[q]), pack, 0)
        c = pltpu.make_async_copy(xout.at[back_span(q)], out.at[back_span(q)], out_sem.at[q])
        c.start()
        stores.append(c)

    for c in stores:
        c.wait()
    for c in shifts[0] + shifts[1] + [occ_shift] + returns[0] + returns[1]:
        c.wait_send()
    for q, z in RELAY_Z.items():
        @pl.when(place == 2 * z + 1)
        def _(q=q):
            for j in range(MEMBERS):
                handed_on(j, q).wait_send()
    for q in range(NQ):
        out_sent(1, q)
        back_sent(1, q)


def per_device(bands, occupations):
    h, second, second_t = (jnp.asarray(t) for t in tables())
    dma = pltpu.SemaphoreType.DMA
    hbm = pl.BlockSpec(memory_space=pl.ANY)
    planes_first = bands.transpose(1, 0, 2)
    total = pl.pallas_call(
        kernel,
        out_shape=jax.ShapeDtypeStruct(planes_first.shape, F32),
        in_specs=[hbm, pl.BlockSpec(memory_space=pltpu.SMEM), hbm, hbm, hbm],
        out_specs=hbm,
        scratch_shapes=[
            pltpu.VMEM((PLANES, MEMBERS, SURFACE), F32),
            pltpu.VMEM((PAD * MEMBERS, PAD), F32),
            pltpu.VMEM((MEMBERS, PLANES, PAD, PAD), BF),
            pltpu.VMEM((MEMBERS, PLANES, PAD, PAD), BF),
            pltpu.VMEM((8, PAD), F32),
            pltpu.VMEM((8, PAD), F32),
            pltpu.VMEM((MEMBERS, ROWS, PAD, PAD), F32),
            pltpu.VMEM((MEMBERS, PLANES, GRID * ROWS, PAD), BF),
            pltpu.VMEM((MEMBERS, NG, ROWS, PAD), BF),
            pltpu.VMEM((PAD * ROWS, PAD), F32),
            pltpu.VMEM((PAD * ROWS, PAD), F32),
            pltpu.VMEM((MEMBERS, NG, ROWS, PAD), BF),
            pltpu.VMEM((MEMBERS, PLANES, GRID * ROWS, PAD), BF),
            pltpu.VMEM((MEMBERS, PLANES, PAD, PAD), F32),
            pltpu.VMEM((MEMBERS, PLANES, PAD, PAD), BF),
            pltpu.VMEM((MEMBERS, PLANES, PAD, PAD), BF),
            pltpu.VMEM((PLANES, MEMBERS, SURFACE), F32),
            pltpu.VMEM(h.shape, BF),
            pltpu.VMEM(second.shape, BF),
            pltpu.VMEM(second_t.shape, BF),
            pltpu.VMEM((MEMBERS, RELAY_PLANES, PAD, PAD), BF),
            dma((NQ,)), dma((3,)), dma((NQ,)),
            dma((MEMBERS, NQ)), dma((MEMBERS, NQ)), dma, dma,
            dma((MEMBERS, NQ)), dma((MEMBERS, NQ)), dma((MEMBERS, NQ)),
            dma((MEMBERS, NQ)), dma((MEMBERS, NQ)), dma((MEMBERS, NQ)),
            dma((MEMBERS, NQ)), dma((MEMBERS, NQ)), dma((MEMBERS,)), dma((MEMBERS,)),
        ],
        compiler_params=pltpu.CompilerParams(
            collective_id=0, has_side_effects=True, vmem_limit_bytes=58 * 2**20),
    )(planes_first, occupations, h, second, second_t)
    return total.transpose(1, 0, 2)


def solution(mesh):
    return jax.shard_map(
        per_device,
        mesh=mesh,
        in_specs=(P("band", "grid", None), P("band")),
        out_specs=P("band", "grid", None),
        check_vma=False,
    )
```

```python
import functools
import math

import jax
import jax.numpy as jnp
import ml_dtypes
import numpy as np
from jax import lax
from jax.experimental import pallas as pl
from jax.experimental.pallas import tpu as pltpu
from jax.sharding import PartitionSpec as P

COULOMB = 160.0
NG = 120
PAD = 128
GRID = 8
PLANES = 15
MEMBERS = 2
ROWS = 32
TILE = 16
OUT_GROUPS = ((0, 3), (3, 5), (8, 7))
BACK_GROUPS = ((0, 7), (7, 5), (12, 3))
NQ = len(OUT_GROUPS)
RELAY_Z = {1: 3, 2: 2}
HAND_ON = {(0, 2): 0, (1, 0): 1}
RETURN_Z = {0: 6, 1: 5, 2: 4}
RELAY_PLANES = max(OUT_GROUPS[q][1] for q in RELAY_Z)
RETURN_PLANES = max(BACK_GROUPS[q][1] for q in RETURN_Z)
SURFACE = NG * NG
MESH = pl.DeviceIdType.MESH
BF = jnp.bfloat16
F32 = jnp.float32


def tables():
    n = np.arange(NG)
    angle = (n[:, None] * n[None, :] % NG).astype(np.float32) * np.float32(2.0 * math.pi / NG)
    h = (np.cos(angle) + np.sin(angle)) / np.float32(math.sqrt(NG))
    padded = np.zeros((PAD, PAD), np.float32)
    padded[:NG, :NG] = h
    second = np.zeros((GRID * ROWS, MEMBERS, PAD), np.float32)
    for p in range(MEMBERS):
        second[p * NG:(p + 1) * NG, p, :NG] = h
    second = second.reshape(GRID * ROWS, MEMBERS * PAD)
    return (
        padded.astype(ml_dtypes.bfloat16),
        second.astype(ml_dtypes.bfloat16),
        np.ascontiguousarray(second.T).astype(ml_dtypes.bfloat16),
    )


def dot(a, b):
    return jnp.dot(a, b, preferred_element_type=F32)


def square(index):
    folded = jnp.where(index <= NG // 2, index, index - NG).astype(F32)
    return folded * folded


def kernel(bands, occ, h_hbm, second_hbm, second_t_hbm, out,
           xin, rows32, own, part, occ_mine, occ_part, coul, send, got, wide, wide2,
           back_send, back, local, ret, ret_got, xout, h_ref, second_ref, second_t_ref, relayed, returned,
           in_sem, c_sem, out_sem, sh_send, sh_recv, oc_send, oc_recv, f_send, f_recv, f_own,
           b_send, b_recv, b_own, r_send, r_recv, re_send, re_recv, rr_send, rr_recv):
    me_b = lax.axis_index("band")
    me = lax.axis_index("grid")
    groups = lax.axis_size("band")
    core = lax.rem(me_b, 2)
    ahead = {"band": lax.rem(me_b + 1, groups)}
    behind = {"band": lax.rem(me_b + groups - 1, groups)}

    side = groups // 2
    column = me_b // side
    place = lax.rem(me_b, side)
    first = place == 0
    last = place == side - 1
    other = (1 - column) * side

    def remote(src, dst, send_sem, recv_sem, to):
        return pltpu.make_async_remote_copy(
            src, dst, send_sem, recv_sem, device_id=to, device_id_type=MESH)

    def out_span(q):
        return pl.ds(*OUT_GROUPS[q])

    def back_span(q):
        return pl.ds(*BACK_GROUPS[q])

    loads = [
        pltpu.make_async_copy(bands.at[out_span(q)], xin.at[out_span(q)], in_sem.at[q]) for q in range(NQ)]
    consts = [
        pltpu.make_async_copy(src, dst, c_sem.at[n])
        for n, (src, dst) in enumerate(
            ((h_hbm, h_ref), (second_hbm, second_ref), (second_t_hbm, second_t_ref)))
    ]
    for c in loads + consts:
        c.start()

    def greet(to):
        pl.semaphore_signal(barrier, inc=1, device_id=to, device_id_type=MESH)

    barrier = pltpu.get_barrier_semaphore()
    for d in range(1, GRID):
        greet({"grid": lax.rem(me + d, GRID)})
    greet(ahead)
    greet(behind)
    greetings = GRID + 1
    for is_source, source, is_target, stops in (
            (last, side - 1, first, [2 * z + 1 for z in RELAY_Z.values()]),
            (first, 0, last, [2 * z for z in RETURN_Z.values()])):
        for stop in stops:
            @pl.when(place == stop)
            def _(source=source):
                greet({"band": other + source})

            @pl.when(is_target)
            def _(stop=stop):
                greet({"band": column * side + stop})
            greetings += (place == stop).astype(jnp.int32)
        greetings += jnp.where(is_source, len(stops), 0)

    lane = lax.broadcasted_iota(jnp.int32, (MEMBERS, PAD), 1)
    rows32[pl.ds(NG * MEMBERS, 8 * MEMBERS), :] = jnp.zeros((8 * MEMBERS, PAD), F32)
    wide[pl.ds(NG * ROWS, 8 * ROWS), :] = jnp.zeros((8 * ROWS, PAD), F32)
    row = lax.broadcasted_iota(jnp.int32, (8, PAD), 0)
    occ_mine[...] = jnp.where(row == 0, occ[0], occ[1])

    def unpack(x, _):
        tiles = {}

        def tile_of(t):
            if t not in tiles:
                if (t + 1) * PAD <= SURFACE:
                    tiles[t] = xin[x, :, t * PAD:(t + 1) * PAD]
                else:
                    half = xin[x, :, t * PAD:SURFACE]
                    tiles[t] = jnp.concatenate([half, jnp.zeros_like(half)], axis=1)
            return tiles[t]

        for r in range(NG):
            tile, off = divmod(NG * r, PAD)
            a = tile_of(tile)
            if off > PAD - NG:
                a = jnp.where(lane >= off, a, tile_of(tile + 1))
            if off:
                a = pltpu.roll(a, PAD - off, 1)
            rows32[pl.ds(r * MEMBERS, MEMBERS), :] = jnp.where(lane < NG, a, 0.0)
        for i in range(MEMBERS):
            own[i, x] = rows32[pl.ds(i, PAD, stride=MEMBERS), :].astype(BF)
        return 0

    shifts = [[
        remote(own.at[j, out_span(q)], part.at[j, out_span(q)], sh_send.at[j, q], sh_recv.at[j, q], ahead)
        for q in range(NQ)] for j in range(MEMBERS)]

    def relay_room(j, q):
        return relayed.at[j, pl.ds(0, OUT_GROUPS[q][1])]

    def start_shift(j, q):
        if q not in RELAY_Z:
            shifts[j][q].start()
            return

        @pl.when(last)
        def _():
            remote(own.at[j, out_span(q)], relay_room(j, q), sh_send.at[j, q], re_recv.at[j],
                   {"band": other + 2 * RELAY_Z[q] + 1}).start()

        @pl.when(jnp.logical_not(last))
        def _():
            shifts[j][q].start()

    def handed_on(j, q):
        return remote(relay_room(j, q), part.at[j, out_span(q)], re_send.at[j], sh_recv.at[j, q],
                      {"band": column * side})

    def hand_on(j):
        for q, z in RELAY_Z.items():
            @pl.when(place == 2 * z + 1)
            def _(q=q):
                remote(relay_room(j, q), relay_room(j, q), re_send.at[j], re_recv.at[j], ahead).wait_recv()
                handed_on(j, q).start()

    def start_return(j, q):
        if j or q not in RETURN_Z:
            returns[j][q].start()
            return

        @pl.when(first)
        def _():
            remote(ret.at[j, back_span(q)], return_room(q), r_send.at[j, q], rr_recv,
                   {"band": other + 2 * RETURN_Z[q]}).start()

        @pl.when(jnp.logical_not(first))
        def _():
            returns[j][q].start()

    def return_room(q):
        return returned.at[pl.ds(0, BACK_GROUPS[q][1])]

    def handed_back(q):
        return remote(return_room(q), ret_got.at[0, back_span(q)], rr_send, r_recv.at[0, q],
                      {"band": column * side + side - 1})

    def hand_back():
        for q, z in RETURN_Z.items():
            @pl.when(place == 2 * z)
            def _(q=q):
                remote(return_room(q), return_room(q), rr_send, rr_recv, ahead).wait_recv()
                handed_back(q).start()

    occ_shift = remote(occ_mine, occ_part, oc_send, oc_recv, ahead)
    for q in range(NQ):
        loads[q].wait()
        lax.fori_loop(OUT_GROUPS[q][0], sum(OUT_GROUPS[q]), unpack, 0)
        if q == 0:
            pl.semaphore_wait(barrier, greetings)
        start_shift(0, q)
    for q in range(NQ):
        start_shift(1, q)
    occ_shift.start()

    lights = [lax.rem(core + j, 2) * (GRID // 2) + 2 * j + core for j in range(MEMBERS)]

    def row_of(j, g):
        return pl.multiple_of(lax.rem(g + 2 * GRID - 1 - lights[j], GRID) * ROWS, ROWS)

    def by_light(is_light, action):
        pl.when(is_light)(functools.partial(action, TILE))
        pl.when(jnp.logical_not(is_light))(functools.partial(action, ROWS))

    for c in consts:
        c.wait()

    def taken(sem, planes, rows):
        view = send.at[0, pl.ds(0, planes), pl.ds(0, rows)]
        remote(view, view, sem, sem, ahead).wait_recv()

    most, full = (GRID - 2) * ROWS + TILE, (GRID - 1) * ROWS

    def out_sent(j, q):
        @pl.when(me == lights[j])
        def _():
            taken(f_send.at[j, q], OUT_GROUPS[q][1], full)

        @pl.when(me != lights[j])
        def _():
            taken(f_send.at[j, q], OUT_GROUPS[q][1], most)

    def back_sent(j, q):
        by_light(me == lights[j], lambda n: taken(b_send.at[j, q], BACK_GROUPS[q][1], (GRID - 1) * n))

    f_mine, b_mine = {}, {}
    for j in range(MEMBERS):
        for q in range(NQ):
            shifts[j][q].wait_recv()

            def forward(x, _, j=j):
                v = part[j, x]
                d = jnp.concatenate([own[0, x] * v, own[1, x] * v], axis=0)
                t = dot(d, h_ref[...]).astype(BF)
                send[j, x] = dot(second_ref[...], t).astype(BF)
                return 0
            lax.fori_loop(OUT_GROUPS[q][0], sum(OUT_GROUPS[q]), forward, 0, unroll=OUT_GROUPS[q][1])
            if j:
                out_sent(0, q)

            there = pl.ds(me * PLANES + OUT_GROUPS[q][0], OUT_GROUPS[q][1])
            f_mine[j, q] = pltpu.make_async_copy(
                send.at[j, out_span(q), pl.ds(row_of(j, me), ROWS)], got.at[j, there], f_own.at[j, q])
            f_mine[j, q].start()
            for d in range(1, GRID):
                to = lax.rem(me + d, GRID)

                def go(n, j=j, q=q, to=to, there=there):
                    remote(send.at[j, out_span(q), pl.ds(row_of(j, to), n)], got.at[j, there, pl.ds(0, n)],
                           f_send.at[j, q], f_recv.at[j, q], {"grid": to}).start()
                by_light(to == lights[j], go)
            if (j, q) in HAND_ON:
                hand_on(HAND_ON[j, q])

    kx = square(lax.broadcasted_iota(jnp.int32, (PAD, PAD), 0))
    kz = square(lax.broadcasted_iota(jnp.int32, (PAD, PAD), 1))
    plane_sq = kx + kz
    for j in range(MEMBERS):
        start = row_of(j, me)

        def fill(l, _, j=j, start=start):
            s = plane_sq + square(lax.rem(start + l, NG))
            coul[j, l] = jnp.where(s > 0.5, COULOMB / jnp.maximum(s, 1.0), 0.0)
            return 0
        lax.fori_loop(0, ROWS, fill, 0)
    for j in range(MEMBERS):
        back[j, :, pl.ds(MEMBERS * NG, TILE)] = jnp.zeros((PLANES, TILE, PAD), BF)
    for j in range(MEMBERS):
        for q in range(NQ):
            f_mine[j, q].wait()
            by_light(me == lights[j],
                     lambda n, j=j, q=q: taken(f_recv.at[j, q], OUT_GROUPS[q][1], (GRID - 1) * n))

        def widen(x, _, j=j):
            wide[pl.ds(pl.multiple_of(x * ROWS, ROWS), ROWS), :] = got[j, x].astype(F32)
            return 0
        lax.fori_loop(0, NG, widen, 0, unroll=8)

        def solve(l, _, j=j):
            r = jnp.concatenate(
                [wide[pl.ds(l, PAD, stride=ROWS), :], wide[pl.ds(TILE + l, PAD, stride=ROWS), :]], axis=1)
            f = dot(h_ref[...], r.astype(BF))
            f = (f * jnp.concatenate([coul[j, l], coul[j, TILE + l]], axis=1)).astype(BF)
            g = dot(h_ref[...], f)
            wide2[pl.ds(l, PAD, stride=ROWS), :] = g[:, :PAD]
            wide2[pl.ds(TILE + l, PAD, stride=ROWS), :] = g[:, PAD:]
            return 0
        lax.fori_loop(0, TILE, solve, 0, unroll=4)

        for q in range(NQ):
            begin, planes = BACK_GROUPS[q]

            def narrow(g, _, j=j, begin=begin, planes=planes):
                for x in range(planes):
                    at = g * PLANES + begin + x
                    back_send[j, at] = wide2[pl.ds(pl.multiple_of(at * ROWS, ROWS), ROWS), :].astype(BF)
                return 0
            lax.fori_loop(0, GRID, narrow, 0, unroll=2)
            if j:
                back_sent(0, q)

            def go(n, j=j, q=q, begin=begin, planes=planes):
                here = back.at[j, back_span(q), pl.ds(row_of(j, me), n)]
                pltpu.make_async_copy(
                    back_send.at[j, pl.ds(me * PLANES + begin, planes), pl.ds(0, n)], here, b_own.at[j, q]).start()
                for d in range(1, GRID):
                    to = lax.rem(me + d, GRID)
                    remote(back_send.at[j, pl.ds(to * PLANES + begin, planes), pl.ds(0, n)], here,
                           b_send.at[j, q], b_recv.at[j, q], {"grid": to}).start()
            by_light(me == lights[j], go)

    def came_back(j, q):
        begin, planes = BACK_GROUPS[q]

        def wait(n):
            view = back_send.at[j, pl.ds(me * PLANES + begin, planes), pl.ds(0, n)]
            pltpu.make_async_copy(view, back.at[j, back_span(q), pl.ds(row_of(j, me), n)], b_own.at[j, q]).wait()
            taken(b_recv.at[j, q], planes, full if n == TILE else most)
        by_light(me == lights[j], wait)

    occ_shift.wait_recv()
    returns = [[
        remote(ret.at[j, back_span(q)], ret_got.at[j, back_span(q)], r_send.at[j, q], r_recv.at[j, q], behind)
        for q in range(NQ)] for j in range(MEMBERS)]
    for j in range(MEMBERS):
        for q in range(NQ):
            came_back(j, q)

            def inverse(x, _, j=j):
                u = dot(second_t_ref[...], back[j, x]).astype(BF)
                v = dot(u, h_ref[...])
                v0, v1 = v[:PAD], v[PAD:]
                w = part[j, x].astype(F32) * occ_part[pl.ds(j, 1), :]
                if j == 0:
                    local[0, x] = -(v0 * w)
                    local[1, x] = -(v1 * w)
                else:
                    local[0, x] -= v0 * w
                    local[1, x] -= v1 * w
                s = (v0 * (own[0, x].astype(F32) * occ_mine[pl.ds(0, 1), :])
                     + v1 * (own[1, x].astype(F32) * occ_mine[pl.ds(1, 1), :]))
                ret[j, x] = (-s).astype(BF)
                return 0
            lax.fori_loop(BACK_GROUPS[q][0], sum(BACK_GROUPS[q]), inverse, 0, unroll=BACK_GROUPS[q][1])
            start_return(j, q)
            if j and q == 1:
                hand_back()

    def pack(x, _):
        for i in range(MEMBERS):
            rows32[pl.ds(i, PAD, stride=MEMBERS), :] = local[i, x] + ret_got[i, x].astype(F32)
        before = None
        for r in range(NG):
            tile = -(-NG * r // PAD)
            begin = PAD * tile - NG * r
            v = rows32[pl.ds(r * MEMBERS, MEMBERS), :]
            if begin:
                v = pltpu.roll(v, PAD - begin, 1)
            if r % 16:
                t = tile - 1
                z0 = PAD * t - NG * (r - 1)
                xout[x, :, t * PAD:(t + 1) * PAD] = jnp.where(lane < NG - z0, before, v)
            before = v
        xout[x, :, SURFACE - 64:] = before[:, :64]
        return 0

    stores = []
    for q in range(NQ):
        for j in range(MEMBERS):
            returns[j][q].wait_recv()
        lax.fori_loop(BACK_GROUPS[q][0], sum(BACK_GROUPS[q]), pack, 0)
        c = pltpu.make_async_copy(xout.at[back_span(q)], out.at[back_span(q)], out_sem.at[q])
        c.start()
        stores.append(c)

    for c in stores:
        c.wait()
    for c in shifts[0] + shifts[1] + [occ_shift] + returns[0] + returns[1]:
        c.wait_send()
    for q, z in RELAY_Z.items():
        @pl.when(place == 2 * z + 1)
        def _(q=q):
            for j in range(MEMBERS):
                handed_on(j, q).wait_send()
    for q, z in RETURN_Z.items():
        @pl.when(place == 2 * z)
        def _(q=q):
            handed_back(q).wait_send()
    for q in range(NQ):
        out_sent(1, q)
        back_sent(1, q)


def per_device(bands, occupations):
    h, second, second_t = (jnp.asarray(t) for t in tables())
    dma = pltpu.SemaphoreType.DMA
    hbm = pl.BlockSpec(memory_space=pl.ANY)
    planes_first = bands.transpose(1, 0, 2)
    total = pl.pallas_call(
        kernel,
        out_shape=jax.ShapeDtypeStruct(planes_first.shape, F32),
        in_specs=[hbm, pl.BlockSpec(memory_space=pltpu.SMEM), hbm, hbm, hbm],
        out_specs=hbm,
        scratch_shapes=[
            pltpu.VMEM((PLANES, MEMBERS, SURFACE), F32),
            pltpu.VMEM((PAD * MEMBERS, PAD), F32),
            pltpu.VMEM((MEMBERS, PLANES, PAD, PAD), BF),
            pltpu.VMEM((MEMBERS, PLANES, PAD, PAD), BF),
            pltpu.VMEM((8, PAD), F32),
            pltpu.VMEM((8, PAD), F32),
            pltpu.VMEM((MEMBERS, ROWS, PAD, PAD), F32),
            pltpu.VMEM((MEMBERS, PLANES, GRID * ROWS, PAD), BF),
            pltpu.VMEM((MEMBERS, NG, ROWS, PAD), BF),
            pltpu.VMEM((PAD * ROWS, PAD), F32),
            pltpu.VMEM((PAD * ROWS, PAD), F32),
            pltpu.VMEM((MEMBERS, NG, ROWS, PAD), BF),
            pltpu.VMEM((MEMBERS, PLANES, GRID * ROWS, PAD), BF),
            pltpu.VMEM((MEMBERS, PLANES, PAD, PAD), F32),
            pltpu.VMEM((MEMBERS, PLANES, PAD, PAD), BF),
            pltpu.VMEM((MEMBERS, PLANES, PAD, PAD), BF),
            pltpu.VMEM((PLANES, MEMBERS, SURFACE), F32),
            pltpu.VMEM(h.shape, BF),
            pltpu.VMEM(second.shape, BF),
            pltpu.VMEM(second_t.shape, BF),
            pltpu.VMEM((MEMBERS, RELAY_PLANES, PAD, PAD), BF),
            pltpu.VMEM((RETURN_PLANES, PAD, PAD), BF),
            dma((NQ,)), dma((3,)), dma((NQ,)),
            dma((MEMBERS, NQ)), dma((MEMBERS, NQ)), dma, dma,
            dma((MEMBERS, NQ)), dma((MEMBERS, NQ)), dma((MEMBERS, NQ)),
            dma((MEMBERS, NQ)), dma((MEMBERS, NQ)), dma((MEMBERS, NQ)),
            dma((MEMBERS, NQ)), dma((MEMBERS, NQ)), dma((MEMBERS,)), dma((MEMBERS,)), dma, dma,
        ],
        compiler_params=pltpu.CompilerParams(
            collective_id=0, has_side_effects=True, vmem_limit_bytes=58 * 2**20),
    )(planes_first, occupations, h, second, second_t)
    return total.transpose(1, 0, 2)


def solution(mesh):
    return jax.shard_map(
        per_device,
        mesh=mesh,
        in_specs=(P("band", "grid", None), P("band")),
        out_specs=P("band", "grid", None),
        check_vma=False,
    )
```

```python
import functools
import math

import jax
import jax.numpy as jnp
import ml_dtypes
import numpy as np
from jax import lax
from jax.experimental import pallas as pl
from jax.experimental.pallas import tpu as pltpu
from jax.sharding import PartitionSpec as P

COULOMB = 160.0
NG = 120
PAD = 128
GRID = 8
PLANES = 15
MEMBERS = 2
ROWS = 32
TILE = 16
OUT_GROUPS = ((0, 3), (3, 5), (8, 7))
BACK_GROUPS = ((0, 7), (7, 5), (12, 3))
NQ = len(OUT_GROUPS)
RELAY_Z = {(0, 1): 3, (0, 2): 2, (1, 1): 4, (1, 2): 1}
HAND_ON = {(0, 2): 0, (1, 1): 1}
RETURN_Z = {0: 6, 1: 5}
RELAY_PLANES = max(OUT_GROUPS[q][1] for _, q in RELAY_Z)
RETURN_PLANES = max(BACK_GROUPS[q][1] for q in RETURN_Z)
SURFACE = NG * NG
MESH = pl.DeviceIdType.MESH
BF = jnp.bfloat16
F32 = jnp.float32


def tables():
    n = np.arange(NG)
    angle = (n[:, None] * n[None, :] % NG).astype(np.float32) * np.float32(2.0 * math.pi / NG)
    h = (np.cos(angle) + np.sin(angle)) / np.float32(math.sqrt(NG))
    padded = np.zeros((PAD, PAD), np.float32)
    padded[:NG, :NG] = h
    second = np.zeros((GRID * ROWS, MEMBERS, PAD), np.float32)
    for p in range(MEMBERS):
        second[p * NG:(p + 1) * NG, p, :NG] = h
    second = second.reshape(GRID * ROWS, MEMBERS * PAD)
    return (
        padded.astype(ml_dtypes.bfloat16),
        second.astype(ml_dtypes.bfloat16),
        np.ascontiguousarray(second.T).astype(ml_dtypes.bfloat16),
    )


def dot(a, b):
    return jnp.dot(a, b, preferred_element_type=F32)


def square(index):
    folded = jnp.where(index <= NG // 2, index, index - NG).astype(F32)
    return folded * folded


def kernel(bands, occ, h_hbm, second_hbm, second_t_hbm, out,
           xin, rows32, own, part, occ_mine, occ_part, coul, send, got, wide, wide2,
           back_send, back, local, ret, ret_got, xout, h_ref, second_ref, second_t_ref, relayed, returned,
           in_sem, c_sem, out_sem, sh_send, sh_recv, oc_send, oc_recv, f_send, f_recv, f_own,
           b_send, b_recv, b_own, r_send, r_recv, re_send, re_recv, rr_send, rr_recv):
    me_b = lax.axis_index("band")
    me = lax.axis_index("grid")
    groups = lax.axis_size("band")
    core = lax.rem(me_b, 2)
    ahead = {"band": lax.rem(me_b + 1, groups)}
    behind = {"band": lax.rem(me_b + groups - 1, groups)}

    side = groups // 2
    column = me_b // side
    place = lax.rem(me_b, side)
    first = place == 0
    last = place == side - 1
    other = (1 - column) * side

    def remote(src, dst, send_sem, recv_sem, to):
        return pltpu.make_async_remote_copy(
            src, dst, send_sem, recv_sem, device_id=to, device_id_type=MESH)

    def out_span(q):
        return pl.ds(*OUT_GROUPS[q])

    def back_span(q):
        return pl.ds(*BACK_GROUPS[q])

    loads = [
        pltpu.make_async_copy(bands.at[out_span(q)], xin.at[out_span(q)], in_sem.at[q]) for q in range(NQ)]
    consts = [
        pltpu.make_async_copy(src, dst, c_sem.at[n])
        for n, (src, dst) in enumerate(
            ((h_hbm, h_ref), (second_hbm, second_ref), (second_t_hbm, second_t_ref)))
    ]
    for c in loads + consts:
        c.start()

    def greet(to):
        pl.semaphore_signal(barrier, inc=1, device_id=to, device_id_type=MESH)

    barrier = pltpu.get_barrier_semaphore()
    for d in range(1, GRID):
        greet({"grid": lax.rem(me + d, GRID)})
    greet(ahead)
    greet(behind)
    greetings = GRID + 1
    for is_source, source, is_target, stops in (
            (last, side - 1, first, [2 * z + 1 for z in RELAY_Z.values()]),
            (first, 0, last, [2 * z for z in RETURN_Z.values()])):
        for stop in stops:
            @pl.when(place == stop)
            def _(source=source):
                greet({"band": other + source})

            @pl.when(is_target)
            def _(stop=stop):
                greet({"band": column * side + stop})
            greetings += (place == stop).astype(jnp.int32)
        greetings += jnp.where(is_source, len(stops), 0)

    lane = lax.broadcasted_iota(jnp.int32, (MEMBERS, PAD), 1)
    rows32[pl.ds(NG * MEMBERS, 8 * MEMBERS), :] = jnp.zeros((8 * MEMBERS, PAD), F32)
    wide[pl.ds(NG * ROWS, 8 * ROWS), :] = jnp.zeros((8 * ROWS, PAD), F32)
    row = lax.broadcasted_iota(jnp.int32, (8, PAD), 0)
    occ_mine[...] = jnp.where(row == 0, occ[0], occ[1])

    def unpack(x, _):
        tiles = {}

        def tile_of(t):
            if t not in tiles:
                if (t + 1) * PAD <= SURFACE:
                    tiles[t] = xin[x, :, t * PAD:(t + 1) * PAD]
                else:
                    half = xin[x, :, t * PAD:SURFACE]
                    tiles[t] = jnp.concatenate([half, jnp.zeros_like(half)], axis=1)
            return tiles[t]

        for r in range(NG):
            tile, off = divmod(NG * r, PAD)
            a = tile_of(tile)
            if off > PAD - NG:
                a = jnp.where(lane >= off, a, tile_of(tile + 1))
            if off:
                a = pltpu.roll(a, PAD - off, 1)
            rows32[pl.ds(r * MEMBERS, MEMBERS), :] = jnp.where(lane < NG, a, 0.0)
        for i in range(MEMBERS):
            own[i, x] = rows32[pl.ds(i, PAD, stride=MEMBERS), :].astype(BF)
        return 0

    shifts = [[
        remote(own.at[j, out_span(q)], part.at[j, out_span(q)], sh_send.at[j, q], sh_recv.at[j, q], ahead)
        for q in range(NQ)] for j in range(MEMBERS)]

    def relay_room(q):
        return relayed.at[pl.ds(0, OUT_GROUPS[q][1])]

    def start_shift(j, q):
        if (j, q) not in RELAY_Z:
            shifts[j][q].start()
            return

        @pl.when(last)
        def _():
            remote(own.at[j, out_span(q)], relay_room(q), sh_send.at[j, q], re_recv,
                   {"band": other + 2 * RELAY_Z[j, q] + 1}).start()

        @pl.when(jnp.logical_not(last))
        def _():
            shifts[j][q].start()

    def handed_on(j, q):
        return remote(relay_room(q), part.at[j, out_span(q)], re_send, sh_recv.at[j, q],
                      {"band": column * side})

    def hand_on(wanted):
        for (j, q), z in RELAY_Z.items():
            if j == wanted:
                @pl.when(place == 2 * z + 1)
                def _(j=j, q=q):
                    remote(relay_room(q), relay_room(q), re_send, re_recv, ahead).wait_recv()
                    handed_on(j, q).start()

    def start_return(j, q):
        if j or q not in RETURN_Z:
            returns[j][q].start()
            return

        @pl.when(first)
        def _():
            remote(ret.at[j, back_span(q)], return_room(q), r_send.at[j, q], rr_recv,
                   {"band": other + 2 * RETURN_Z[q]}).start()

        @pl.when(jnp.logical_not(first))
        def _():
            returns[j][q].start()

    def return_room(q):
        return returned.at[pl.ds(0, BACK_GROUPS[q][1])]

    def handed_back(q):
        return remote(return_room(q), ret_got.at[0, back_span(q)], rr_send, r_recv.at[0, q],
                      {"band": column * side + side - 1})

    def hand_back():
        for q, z in RETURN_Z.items():
            @pl.when(place == 2 * z)
            def _(q=q):
                remote(return_room(q), return_room(q), rr_send, rr_recv, ahead).wait_recv()
                handed_back(q).start()

    occ_shift = remote(occ_mine, occ_part, oc_send, oc_recv, ahead)
    for q in range(NQ):
        loads[q].wait()
        lax.fori_loop(OUT_GROUPS[q][0], sum(OUT_GROUPS[q]), unpack, 0)
        if q == 0:
            pl.semaphore_wait(barrier, greetings)
        start_shift(0, q)
    for q in range(NQ):
        start_shift(1, q)
    occ_shift.start()

    lights = [lax.rem(core + j, 2) * (GRID // 2) + 2 * j + core for j in range(MEMBERS)]

    def row_of(j, g):
        return pl.multiple_of(lax.rem(g + 2 * GRID - 1 - lights[j], GRID) * ROWS, ROWS)

    def by_light(is_light, action):
        pl.when(is_light)(functools.partial(action, TILE))
        pl.when(jnp.logical_not(is_light))(functools.partial(action, ROWS))

    for c in consts:
        c.wait()

    def taken(sem, planes, rows):
        view = send.at[0, pl.ds(0, planes), pl.ds(0, rows)]
        remote(view, view, sem, sem, ahead).wait_recv()

    most, full = (GRID - 2) * ROWS + TILE, (GRID - 1) * ROWS

    def out_sent(j, q):
        @pl.when(me == lights[j])
        def _():
            taken(f_send.at[j, q], OUT_GROUPS[q][1], full)

        @pl.when(me != lights[j])
        def _():
            taken(f_send.at[j, q], OUT_GROUPS[q][1], most)

    def back_sent(j, q):
        by_light(me == lights[j], lambda n: taken(b_send.at[j, q], BACK_GROUPS[q][1], (GRID - 1) * n))

    f_mine, b_mine = {}, {}
    for j in range(MEMBERS):
        for q in range(NQ):
            shifts[j][q].wait_recv()

            def forward(x, _, j=j):
                v = part[j, x]
                d = jnp.concatenate([own[0, x] * v, own[1, x] * v], axis=0)
                t = dot(d, h_ref[...]).astype(BF)
                send[j, x] = dot(second_ref[...], t).astype(BF)
                return 0
            lax.fori_loop(OUT_GROUPS[q][0], sum(OUT_GROUPS[q]), forward, 0, unroll=OUT_GROUPS[q][1])
            if j:
                out_sent(0, q)

            there = pl.ds(me * PLANES + OUT_GROUPS[q][0], OUT_GROUPS[q][1])
            f_mine[j, q] = pltpu.make_async_copy(
                send.at[j, out_span(q), pl.ds(row_of(j, me), ROWS)], got.at[j, there], f_own.at[j, q])
            f_mine[j, q].start()
            for d in range(1, GRID):
                to = lax.rem(me + d, GRID)

                def go(n, j=j, q=q, to=to, there=there):
                    remote(send.at[j, out_span(q), pl.ds(row_of(j, to), n)], got.at[j, there, pl.ds(0, n)],
                           f_send.at[j, q], f_recv.at[j, q], {"grid": to}).start()
                by_light(to == lights[j], go)
            if (j, q) in HAND_ON:
                hand_on(HAND_ON[j, q])

    kx = square(lax.broadcasted_iota(jnp.int32, (PAD, PAD), 0))
    kz = square(lax.broadcasted_iota(jnp.int32, (PAD, PAD), 1))
    plane_sq = kx + kz
    for j in range(MEMBERS):
        start = row_of(j, me)

        def fill(l, _, j=j, start=start):
            s = plane_sq + square(lax.rem(start + l, NG))
            coul[j, l] = jnp.where(s > 0.5, COULOMB / jnp.maximum(s, 1.0), 0.0)
            return 0
        lax.fori_loop(0, ROWS, fill, 0)
    for j in range(MEMBERS):
        back[j, :, pl.ds(MEMBERS * NG, TILE)] = jnp.zeros((PLANES, TILE, PAD), BF)
    for j in range(MEMBERS):
        for q in range(NQ):
            f_mine[j, q].wait()
            by_light(me == lights[j],
                     lambda n, j=j, q=q: taken(f_recv.at[j, q], OUT_GROUPS[q][1], (GRID - 1) * n))

        def widen(x, _, j=j):
            wide[pl.ds(pl.multiple_of(x * ROWS, ROWS), ROWS), :] = got[j, x].astype(F32)
            return 0
        lax.fori_loop(0, NG, widen, 0, unroll=8)

        def solve(l, _, j=j):
            r = jnp.concatenate(
                [wide[pl.ds(l, PAD, stride=ROWS), :], wide[pl.ds(TILE + l, PAD, stride=ROWS), :]], axis=1)
            f = dot(h_ref[...], r.astype(BF))
            f = (f * jnp.concatenate([coul[j, l], coul[j, TILE + l]], axis=1)).astype(BF)
            g = dot(h_ref[...], f)
            wide2[pl.ds(l, PAD, stride=ROWS), :] = g[:, :PAD]
            wide2[pl.ds(TILE + l, PAD, stride=ROWS), :] = g[:, PAD:]
            return 0
        lax.fori_loop(0, TILE, solve, 0, unroll=4)

        for q in range(NQ):
            begin, planes = BACK_GROUPS[q]

            def narrow(g, _, j=j, begin=begin, planes=planes):
                for x in range(planes):
                    at = g * PLANES + begin + x
                    back_send[j, at] = wide2[pl.ds(pl.multiple_of(at * ROWS, ROWS), ROWS), :].astype(BF)
                return 0
            lax.fori_loop(0, GRID, narrow, 0, unroll=2)
            if j:
                back_sent(0, q)

            def go(n, j=j, q=q, begin=begin, planes=planes):
                here = back.at[j, back_span(q), pl.ds(row_of(j, me), n)]
                pltpu.make_async_copy(
                    back_send.at[j, pl.ds(me * PLANES + begin, planes), pl.ds(0, n)], here, b_own.at[j, q]).start()
                for d in range(1, GRID):
                    to = lax.rem(me + d, GRID)
                    remote(back_send.at[j, pl.ds(to * PLANES + begin, planes), pl.ds(0, n)], here,
                           b_send.at[j, q], b_recv.at[j, q], {"grid": to}).start()
            by_light(me == lights[j], go)

    def came_back(j, q):
        begin, planes = BACK_GROUPS[q]

        def wait(n):
            view = back_send.at[j, pl.ds(me * PLANES + begin, planes), pl.ds(0, n)]
            pltpu.make_async_copy(view, back.at[j, back_span(q), pl.ds(row_of(j, me), n)], b_own.at[j, q]).wait()
            taken(b_recv.at[j, q], planes, full if n == TILE else most)
        by_light(me == lights[j], wait)

    occ_shift.wait_recv()
    returns = [[
        remote(ret.at[j, back_span(q)], ret_got.at[j, back_span(q)], r_send.at[j, q], r_recv.at[j, q], behind)
        for q in range(NQ)] for j in range(MEMBERS)]
    for j in range(MEMBERS):
        for q in range(NQ):
            came_back(j, q)

            def inverse(x, _, j=j):
                u = dot(second_t_ref[...], back[j, x]).astype(BF)
                v = dot(u, h_ref[...])
                v0, v1 = v[:PAD], v[PAD:]
                w = part[j, x].astype(F32) * occ_part[pl.ds(j, 1), :]
                if j == 0:
                    local[0, x] = -(v0 * w)
                    local[1, x] = -(v1 * w)
                else:
                    local[0, x] -= v0 * w
                    local[1, x] -= v1 * w
                s = (v0 * (own[0, x].astype(F32) * occ_mine[pl.ds(0, 1), :])
                     + v1 * (own[1, x].astype(F32) * occ_mine[pl.ds(1, 1), :]))
                ret[j, x] = (-s).astype(BF)
                return 0
            lax.fori_loop(BACK_GROUPS[q][0], sum(BACK_GROUPS[q]), inverse, 0, unroll=BACK_GROUPS[q][1])
            start_return(j, q)
            if j and q == 1:
                hand_back()

    def pack(x, _):
        for i in range(MEMBERS):
            rows32[pl.ds(i, PAD, stride=MEMBERS), :] = local[i, x] + ret_got[i, x].astype(F32)
        before = None
        for r in range(NG):
            tile = -(-NG * r // PAD)
            begin = PAD * tile - NG * r
            v = rows32[pl.ds(r * MEMBERS, MEMBERS), :]
            if begin:
                v = pltpu.roll(v, PAD - begin, 1)
            if r % 16:
                t = tile - 1
                z0 = PAD * t - NG * (r - 1)
                xout[x, :, t * PAD:(t + 1) * PAD] = jnp.where(lane < NG - z0, before, v)
            before = v
        xout[x, :, SURFACE - 64:] = before[:, :64]
        return 0

    stores = []
    for q in range(NQ):
        for j in range(MEMBERS):
            returns[j][q].wait_recv()
        lax.fori_loop(BACK_GROUPS[q][0], sum(BACK_GROUPS[q]), pack, 0)
        c = pltpu.make_async_copy(xout.at[back_span(q)], out.at[back_span(q)], out_sem.at[q])
        c.start()
        stores.append(c)

    for c in stores:
        c.wait()
    for c in shifts[0] + shifts[1] + [occ_shift] + returns[0] + returns[1]:
        c.wait_send()
    for (j, q), z in RELAY_Z.items():
        @pl.when(place == 2 * z + 1)
        def _(j=j, q=q):
            handed_on(j, q).wait_send()
    for q, z in RETURN_Z.items():
        @pl.when(place == 2 * z)
        def _(q=q):
            handed_back(q).wait_send()
    for q in range(NQ):
        out_sent(1, q)
        back_sent(1, q)


def pass_on(steps, src, dst, held, in_sem, out_sem):
    planes = PLANES // steps
    spans = [pl.ds(n * planes, planes) for n in range(steps)]
    loads = [pltpu.make_async_copy(src.at[p], held.at[p], in_sem.at[n]) for n, p in enumerate(spans)]
    stores = [pltpu.make_async_copy(held.at[p], dst.at[p], out_sem.at[n]) for n, p in enumerate(spans)]
    for c in loads:
        c.start()
    for load, store in zip(loads, stores):
        load.wait()
        store.start()
    for c in stores:
        c.wait()


def per_device(bands, occupations):
    h, second, second_t = (jnp.asarray(t) for t in tables())
    dma = pltpu.SemaphoreType.DMA
    hbm = pl.BlockSpec(memory_space=pl.ANY)
    planes_first = bands.transpose(1, 0, 2)
    total = pl.pallas_call(
        kernel,
        out_shape=jax.ShapeDtypeStruct(planes_first.shape, F32),
        in_specs=[hbm, pl.BlockSpec(memory_space=pltpu.SMEM), hbm, hbm, hbm],
        out_specs=hbm,
        scratch_shapes=[
            pltpu.VMEM((PLANES, MEMBERS, SURFACE), F32),
            pltpu.VMEM((PAD * MEMBERS, PAD), F32),
            pltpu.VMEM((MEMBERS, PLANES, PAD, PAD), BF),
            pltpu.VMEM((MEMBERS, PLANES, PAD, PAD), BF),
            pltpu.VMEM((8, PAD), F32),
            pltpu.VMEM((8, PAD), F32),
            pltpu.VMEM((MEMBERS, ROWS, PAD, PAD), F32),
            pltpu.VMEM((MEMBERS, PLANES, GRID * ROWS, PAD), BF),
            pltpu.VMEM((MEMBERS, NG, ROWS, PAD), BF),
            pltpu.VMEM((PAD * ROWS, PAD), F32),
            pltpu.VMEM((PAD * ROWS, PAD), F32),
            pltpu.VMEM((MEMBERS, NG, ROWS, PAD), BF),
            pltpu.VMEM((MEMBERS, PLANES, GRID * ROWS, PAD), BF),
            pltpu.VMEM((MEMBERS, PLANES, PAD, PAD), F32),
            pltpu.VMEM((MEMBERS, PLANES, PAD, PAD), BF),
            pltpu.VMEM((MEMBERS, PLANES, PAD, PAD), BF),
            pltpu.VMEM((PLANES, MEMBERS, SURFACE), F32),
            pltpu.VMEM(h.shape, BF),
            pltpu.VMEM(second.shape, BF),
            pltpu.VMEM(second_t.shape, BF),
            pltpu.VMEM((RELAY_PLANES, PAD, PAD), BF),
            pltpu.VMEM((RETURN_PLANES, PAD, PAD), BF),
            dma((NQ,)), dma((3,)), dma((NQ,)),
            dma((MEMBERS, NQ)), dma((MEMBERS, NQ)), dma, dma,
            dma((MEMBERS, NQ)), dma((MEMBERS, NQ)), dma((MEMBERS, NQ)),
            dma((MEMBERS, NQ)), dma((MEMBERS, NQ)), dma((MEMBERS, NQ)),
            dma((MEMBERS, NQ)), dma((MEMBERS, NQ)), dma, dma, dma, dma,
        ],
        compiler_params=pltpu.CompilerParams(
            collective_id=0, has_side_effects=True, vmem_limit_bytes=58 * 2**20),
    )(planes_first, occupations, h, second, second_t)
    steps = 5
    total = pl.pallas_call(
        functools.partial(pass_on, steps),
        out_shape=jax.ShapeDtypeStruct(planes_first.shape, F32),
        in_specs=[hbm],
        out_specs=hbm,
        scratch_shapes=[pltpu.VMEM(planes_first.shape, F32), dma((steps,)), dma((steps,))],
        compiler_params=pltpu.CompilerParams(vmem_limit_bytes=58 * 2**20),
    )(total)
    return total.transpose(1, 0, 2)


def solution(mesh):
    return jax.shard_map(
        per_device,
        mesh=mesh,
        in_specs=(P("band", "grid", None), P("band")),
        out_specs=P("band", "grid", None),
        check_vma=False,
    )
```

```python
import functools
import math

import jax
import jax.numpy as jnp
import ml_dtypes
import numpy as np
from jax import lax
from jax.experimental import pallas as pl
from jax.experimental.pallas import tpu as pltpu
from jax.sharding import PartitionSpec as P

COULOMB = 160.0
NG = 120
PAD = 128
GRID = 8
PLANES = 15
MEMBERS = 2
ROWS = 32
TILE = 16
OUT_GROUPS = ((0, 3), (3, 5), (8, 7))
BACK_GROUPS = ((0, 7), (7, 5), (12, 3))
NQ = len(OUT_GROUPS)
EARLY = 2
RELAY_Z = {(0, 1): 3, (0, 2): 2, (1, 1): 4, (1, 2): 1}
HAND_ON = {(0, 2): 0, (1, 1): 1}
RETURN_Z = {0: 6, 1: 5}
RELAY_PLANES = max(OUT_GROUPS[q][1] for _, q in RELAY_Z)
RETURN_PLANES = max(BACK_GROUPS[q][1] for q in RETURN_Z)
SURFACE = NG * NG
MESH = pl.DeviceIdType.MESH
BF = jnp.bfloat16
F32 = jnp.float32


def tables():
    n = np.arange(NG)
    angle = (n[:, None] * n[None, :] % NG).astype(np.float32) * np.float32(2.0 * math.pi / NG)
    h = (np.cos(angle) + np.sin(angle)) / np.float32(math.sqrt(NG))
    padded = np.zeros((PAD, PAD), np.float32)
    padded[:NG, :NG] = h
    second = np.zeros((GRID * ROWS, MEMBERS, PAD), np.float32)
    for p in range(MEMBERS):
        second[p * NG:(p + 1) * NG, p, :NG] = h
    second = second.reshape(GRID * ROWS, MEMBERS * PAD)
    return (
        padded.astype(ml_dtypes.bfloat16),
        second.astype(ml_dtypes.bfloat16),
        np.ascontiguousarray(second.T).astype(ml_dtypes.bfloat16),
    )


def dot(a, b):
    return jnp.dot(a, b, preferred_element_type=F32)


def square(index):
    folded = jnp.where(index <= NG // 2, index, index - NG).astype(F32)
    return folded * folded


def kernel(bands, occ, h_hbm, second_hbm, second_t_hbm, out,
           xin, rows32, own, part, occ_mine, occ_part, coul, send, got, wide, wide2,
           back_send, back, local, ret, ret_got, xout, h_ref, second_ref, second_t_ref, relayed, returned,
           in_sem, c_sem, out_sem, sh_send, sh_recv, oc_send, oc_recv, f_send, f_recv, f_own,
           b_send, b_recv, b_own, r_send, r_recv, re_send, re_recv, rr_send, rr_recv):
    me_b = lax.axis_index("band")
    me = lax.axis_index("grid")
    groups = lax.axis_size("band")
    core = lax.rem(me_b, 2)
    ahead = {"band": lax.rem(me_b + 1, groups)}
    behind = {"band": lax.rem(me_b + groups - 1, groups)}

    side = groups // 2
    column = me_b // side
    place = lax.rem(me_b, side)
    first = place == 0
    last = place == side - 1
    other = (1 - column) * side

    def remote(src, dst, send_sem, recv_sem, to):
        return pltpu.make_async_remote_copy(
            src, dst, send_sem, recv_sem, device_id=to, device_id_type=MESH)

    def out_span(q):
        return pl.ds(*OUT_GROUPS[q])

    def back_span(q):
        return pl.ds(*BACK_GROUPS[q])

    loads = [
        pltpu.make_async_copy(bands.at[out_span(q)], xin.at[out_span(q)], in_sem.at[q]) for q in range(NQ)]
    consts = [
        pltpu.make_async_copy(src, dst, c_sem.at[n])
        for n, (src, dst) in enumerate(
            ((h_hbm, h_ref), (second_hbm, second_ref), (second_t_hbm, second_t_ref)))
    ]
    for c in loads + consts:
        c.start()

    def greet(to):
        pl.semaphore_signal(barrier, inc=1, device_id=to, device_id_type=MESH)

    barrier = pltpu.get_barrier_semaphore()
    for d in range(1, GRID):
        greet({"grid": lax.rem(me + d, GRID)})
    greet(ahead)
    greet(behind)
    greetings = GRID + 1
    for is_source, source, is_target, stops in (
            (last, side - 1, first, [2 * z + 1 for z in RELAY_Z.values()]),
            (first, 0, last, [2 * z for z in RETURN_Z.values()])):
        for stop in stops:
            @pl.when(place == stop)
            def _(source=source):
                greet({"band": other + source})

            @pl.when(is_target)
            def _(stop=stop):
                greet({"band": column * side + stop})
            greetings += (place == stop).astype(jnp.int32)
        greetings += jnp.where(is_source, len(stops), 0)

    lane = lax.broadcasted_iota(jnp.int32, (MEMBERS, PAD), 1)
    rows32[pl.ds(NG * MEMBERS, 8 * MEMBERS), :] = jnp.zeros((8 * MEMBERS, PAD), F32)
    wide[pl.ds(NG * ROWS, 8 * ROWS), :] = jnp.zeros((8 * ROWS, PAD), F32)
    row = lax.broadcasted_iota(jnp.int32, (8, PAD), 0)
    occ_mine[...] = jnp.where(row == 0, occ[0], occ[1])

    def unpack(x, _):
        tiles = {}

        def tile_of(t):
            if t not in tiles:
                if (t + 1) * PAD <= SURFACE:
                    tiles[t] = xin[x, :, t * PAD:(t + 1) * PAD]
                else:
                    half = xin[x, :, t * PAD:SURFACE]
                    tiles[t] = jnp.concatenate([half, jnp.zeros_like(half)], axis=1)
            return tiles[t]

        for r in range(NG):
            tile, off = divmod(NG * r, PAD)
            a = tile_of(tile)
            if off > PAD - NG:
                a = jnp.where(lane >= off, a, tile_of(tile + 1))
            if off:
                a = pltpu.roll(a, PAD - off, 1)
            rows32[pl.ds(r * MEMBERS, MEMBERS), :] = a
        for i in range(MEMBERS):
            own[i, x] = rows32[pl.ds(i, PAD, stride=MEMBERS), :].astype(BF)
        return 0

    shifts = [[
        remote(own.at[j, out_span(q)], part.at[j, out_span(q)], sh_send.at[j, q], sh_recv.at[j, q], ahead)
        for q in range(NQ)] for j in range(MEMBERS)]

    def relay_room(q):
        return relayed.at[pl.ds(0, OUT_GROUPS[q][1])]

    def start_shift(j, q):
        if (j, q) not in RELAY_Z:
            shifts[j][q].start()
            return

        @pl.when(last)
        def _():
            remote(own.at[j, out_span(q)], relay_room(q), sh_send.at[j, q], re_recv,
                   {"band": other + 2 * RELAY_Z[j, q] + 1}).start()

        @pl.when(jnp.logical_not(last))
        def _():
            shifts[j][q].start()

    def handed_on(j, q):
        return remote(relay_room(q), part.at[j, out_span(q)], re_send, sh_recv.at[j, q],
                      {"band": column * side})

    def hand_on(wanted):
        for (j, q), z in RELAY_Z.items():
            if j == wanted:
                @pl.when(place == 2 * z + 1)
                def _(j=j, q=q):
                    remote(relay_room(q), relay_room(q), re_send, re_recv, ahead).wait_recv()
                    handed_on(j, q).start()

    def start_return(j, q):
        if j or q not in RETURN_Z:
            returns[j][q].start()
            return

        @pl.when(first)
        def _():
            remote(ret.at[j, back_span(q)], return_room(q), r_send.at[j, q], rr_recv,
                   {"band": other + 2 * RETURN_Z[q]}).start()

        @pl.when(jnp.logical_not(first))
        def _():
            returns[j][q].start()

    def return_room(q):
        return returned.at[pl.ds(0, BACK_GROUPS[q][1])]

    def handed_back(q):
        return remote(return_room(q), ret_got.at[0, back_span(q)], rr_send, r_recv.at[0, q],
                      {"band": column * side + side - 1})

    def hand_back():
        for q, z in RETURN_Z.items():
            @pl.when(place == 2 * z)
            def _(q=q):
                remote(return_room(q), return_room(q), rr_send, rr_recv, ahead).wait_recv()
                handed_back(q).start()

    occ_shift = remote(occ_mine, occ_part, oc_send, oc_recv, ahead)
    lights = [lax.rem(core + j, 2) * (GRID // 2) + 2 * j + core for j in range(MEMBERS)]

    def row_of(j, g):
        return pl.multiple_of(lax.rem(g + 2 * GRID - 1 - lights[j], GRID) * ROWS, ROWS)

    def by_light(is_light, action):
        pl.when(is_light)(functools.partial(action, TILE))
        pl.when(jnp.logical_not(is_light))(functools.partial(action, ROWS))

    def taken(sem, planes, rows):
        view = send.at[0, pl.ds(0, planes), pl.ds(0, rows)]
        remote(view, view, sem, sem, ahead).wait_recv()

    most, full = (GRID - 2) * ROWS + TILE, (GRID - 1) * ROWS

    def out_sent(j, q):
        @pl.when(me == lights[j])
        def _():
            taken(f_send.at[j, q], OUT_GROUPS[q][1], full)

        @pl.when(me != lights[j])
        def _():
            taken(f_send.at[j, q], OUT_GROUPS[q][1], most)

    def back_sent(j, q):
        by_light(me == lights[j], lambda n: taken(b_send.at[j, q], BACK_GROUPS[q][1], (GRID - 1) * n))

    f_mine = {}

    def advance(j, q):
        shifts[j][q].wait_recv()

        def forward(x, _):
            v = part[j, x]
            d = jnp.concatenate([own[0, x] * v, own[1, x] * v], axis=0)
            t = dot(d, h_ref[...]).astype(BF)
            send[j, x] = dot(second_ref[...], t).astype(BF)
            return 0
        lax.fori_loop(OUT_GROUPS[q][0], sum(OUT_GROUPS[q]), forward, 0, unroll=OUT_GROUPS[q][1])
        if j:
            out_sent(0, q)

        there = pl.ds(me * PLANES + OUT_GROUPS[q][0], OUT_GROUPS[q][1])
        f_mine[j, q] = pltpu.make_async_copy(
            send.at[j, out_span(q), pl.ds(row_of(j, me), ROWS)], got.at[j, there], f_own.at[j, q])
        f_mine[j, q].start()
        for d in range(1, GRID):
            to = lax.rem(me + d, GRID)

            def go(n, to=to):
                remote(send.at[j, out_span(q), pl.ds(row_of(j, to), n)], got.at[j, there, pl.ds(0, n)],
                       f_send.at[j, q], f_recv.at[j, q], {"grid": to}).start()
            by_light(to == lights[j], go)
        if (j, q) in HAND_ON:
            hand_on(HAND_ON[j, q])

    for q in range(NQ):
        loads[q].wait()
        lax.fori_loop(OUT_GROUPS[q][0], sum(OUT_GROUPS[q]), unpack, 0)
        if q == 0:
            pl.semaphore_wait(barrier, greetings)
        start_shift(0, q)
        if q == EARLY:
            for c in consts:
                c.wait()
            advance(0, 0)
    for q in range(NQ):
        start_shift(1, q)
    occ_shift.start()
    for j in range(MEMBERS):
        for q in range(NQ):
            if j or q:
                advance(j, q)

    kx = square(lax.broadcasted_iota(jnp.int32, (PAD, PAD), 0))
    kz = square(lax.broadcasted_iota(jnp.int32, (PAD, PAD), 1))
    plane_sq = kx + kz
    for j in range(MEMBERS):
        start = row_of(j, me)

        def fill(l, _, j=j, start=start):
            s = plane_sq + square(lax.rem(start + l, NG))
            coul[j, l] = jnp.where(s > 0.5, COULOMB / jnp.maximum(s, 1.0), 0.0)
            return 0
        lax.fori_loop(0, ROWS, fill, 0)
    for j in range(MEMBERS):
        back[j, :, pl.ds(MEMBERS * NG, TILE)] = jnp.zeros((PLANES, TILE, PAD), BF)
    for j in range(MEMBERS):
        for q in range(NQ):
            f_mine[j, q].wait()
            by_light(me == lights[j],
                     lambda n, j=j, q=q: taken(f_recv.at[j, q], OUT_GROUPS[q][1], (GRID - 1) * n))

        def widen(x, _, j=j):
            wide[pl.ds(pl.multiple_of(x * ROWS, ROWS), ROWS), :] = got[j, x].astype(F32)
            return 0
        lax.fori_loop(0, NG, widen, 0, unroll=8)

        def solve(l, _, j=j):
            r = jnp.concatenate(
                [wide[pl.ds(l, PAD, stride=ROWS), :], wide[pl.ds(TILE + l, PAD, stride=ROWS), :]], axis=1)
            f = dot(h_ref[...], r.astype(BF))
            f = (f * jnp.concatenate([coul[j, l], coul[j, TILE + l]], axis=1)).astype(BF)
            g = dot(h_ref[...], f)
            wide2[pl.ds(l, PAD, stride=ROWS), :] = g[:, :PAD]
            wide2[pl.ds(TILE + l, PAD, stride=ROWS), :] = g[:, PAD:]
            return 0
        lax.fori_loop(0, TILE, solve, 0, unroll=4)

        for q in range(NQ):
            begin, planes = BACK_GROUPS[q]

            def narrow(g, _, j=j, begin=begin, planes=planes):
                for x in range(planes):
                    at = g * PLANES + begin + x
                    back_send[j, at] = wide2[pl.ds(pl.multiple_of(at * ROWS, ROWS), ROWS), :].astype(BF)
                return 0
            lax.fori_loop(0, GRID, narrow, 0, unroll=2)
            if j:
                back_sent(0, q)

            def go(n, j=j, q=q, begin=begin, planes=planes):
                here = back.at[j, back_span(q), pl.ds(row_of(j, me), n)]
                pltpu.make_async_copy(
                    back_send.at[j, pl.ds(me * PLANES + begin, planes), pl.ds(0, n)], here, b_own.at[j, q]).start()
                for d in range(1, GRID):
                    to = lax.rem(me + d, GRID)
                    remote(back_send.at[j, pl.ds(to * PLANES + begin, planes), pl.ds(0, n)], here,
                           b_send.at[j, q], b_recv.at[j, q], {"grid": to}).start()
            by_light(me == lights[j], go)

    def came_back(j, q):
        begin, planes = BACK_GROUPS[q]

        def wait(n):
            view = back_send.at[j, pl.ds(me * PLANES + begin, planes), pl.ds(0, n)]
            pltpu.make_async_copy(view, back.at[j, back_span(q), pl.ds(row_of(j, me), n)], b_own.at[j, q]).wait()
            taken(b_recv.at[j, q], planes, full if n == TILE else most)
        by_light(me == lights[j], wait)

    occ_shift.wait_recv()
    returns = [[
        remote(ret.at[j, back_span(q)], ret_got.at[j, back_span(q)], r_send.at[j, q], r_recv.at[j, q], behind)
        for q in range(NQ)] for j in range(MEMBERS)]
    for j in range(MEMBERS):
        for q in range(NQ):
            came_back(j, q)

            def inverse(x, _, j=j):
                u = dot(second_t_ref[...], back[j, x]).astype(BF)
                v = dot(u, h_ref[...])
                v0, v1 = v[:PAD], v[PAD:]
                w = part[j, x].astype(F32) * occ_part[pl.ds(j, 1), :]
                if j == 0:
                    local[0, x] = -(v0 * w)
                    local[1, x] = -(v1 * w)
                else:
                    local[0, x] -= v0 * w
                    local[1, x] -= v1 * w
                s = (v0 * (own[0, x].astype(F32) * occ_mine[pl.ds(0, 1), :])
                     + v1 * (own[1, x].astype(F32) * occ_mine[pl.ds(1, 1), :]))
                ret[j, x] = (-s).astype(BF)
                return 0
            lax.fori_loop(BACK_GROUPS[q][0], sum(BACK_GROUPS[q]), inverse, 0, unroll=BACK_GROUPS[q][1])
            start_return(j, q)
            if j and q == 1:
                hand_back()

    def pack(x, _):
        for i in range(MEMBERS):
            rows32[pl.ds(i, PAD, stride=MEMBERS), :] = local[i, x] + ret_got[i, x].astype(F32)
        before = None
        for r in range(NG):
            tile = -(-NG * r // PAD)
            begin = PAD * tile - NG * r
            v = rows32[pl.ds(r * MEMBERS, MEMBERS), :]
            if begin:
                v = pltpu.roll(v, PAD - begin, 1)
            if r % 16:
                t = tile - 1
                z0 = PAD * t - NG * (r - 1)
                xout[x, :, t * PAD:(t + 1) * PAD] = jnp.where(lane < NG - z0, before, v)
            before = v
        xout[x, :, SURFACE - 64:] = before[:, :64]
        return 0

    stores = []
    for q in range(NQ):
        for j in range(MEMBERS):
            returns[j][q].wait_recv()
        lax.fori_loop(BACK_GROUPS[q][0], sum(BACK_GROUPS[q]), pack, 0)
        c = pltpu.make_async_copy(xout.at[back_span(q)], out.at[back_span(q)], out_sem.at[q])
        c.start()
        stores.append(c)

    for c in stores:
        c.wait()
    for c in shifts[0] + shifts[1] + [occ_shift] + returns[0] + returns[1]:
        c.wait_send()
    for (j, q), z in RELAY_Z.items():
        @pl.when(place == 2 * z + 1)
        def _(j=j, q=q):
            handed_on(j, q).wait_send()
    for q, z in RETURN_Z.items():
        @pl.when(place == 2 * z)
        def _(q=q):
            handed_back(q).wait_send()
    for q in range(NQ):
        out_sent(1, q)
        back_sent(1, q)


def pass_on(steps, src, dst, held, in_sem, out_sem):
    planes = PLANES // steps
    spans = [pl.ds(n * planes, planes) for n in range(steps)]
    loads = [pltpu.make_async_copy(src.at[p], held.at[p], in_sem.at[n]) for n, p in enumerate(spans)]
    stores = [pltpu.make_async_copy(held.at[p], dst.at[p], out_sem.at[n]) for n, p in enumerate(spans)]
    for c in loads:
        c.start()
    for load, store in zip(loads, stores):
        load.wait()
        store.start()
    for c in stores:
        c.wait()


def per_device(bands, occupations):
    h, second, second_t = (jnp.asarray(t) for t in tables())
    dma = pltpu.SemaphoreType.DMA
    hbm = pl.BlockSpec(memory_space=pl.ANY)
    planes_first = bands.transpose(1, 0, 2)
    total = pl.pallas_call(
        kernel,
        out_shape=jax.ShapeDtypeStruct(planes_first.shape, F32),
        in_specs=[hbm, pl.BlockSpec(memory_space=pltpu.SMEM), hbm, hbm, hbm],
        out_specs=hbm,
        scratch_shapes=[
            pltpu.VMEM((PLANES, MEMBERS, SURFACE), F32),
            pltpu.VMEM((PAD * MEMBERS, PAD), F32),
            pltpu.VMEM((MEMBERS, PLANES, PAD, PAD), BF),
            pltpu.VMEM((MEMBERS, PLANES, PAD, PAD), BF),
            pltpu.VMEM((8, PAD), F32),
            pltpu.VMEM((8, PAD), F32),
            pltpu.VMEM((MEMBERS, ROWS, PAD, PAD), F32),
            pltpu.VMEM((MEMBERS, PLANES, GRID * ROWS, PAD), BF),
            pltpu.VMEM((MEMBERS, NG, ROWS, PAD), BF),
            pltpu.VMEM((PAD * ROWS, PAD), F32),
            pltpu.VMEM((PAD * ROWS, PAD), F32),
            pltpu.VMEM((MEMBERS, NG, ROWS, PAD), BF),
            pltpu.VMEM((MEMBERS, PLANES, GRID * ROWS, PAD), BF),
            pltpu.VMEM((MEMBERS, PLANES, PAD, PAD), F32),
            pltpu.VMEM((MEMBERS, PLANES, PAD, PAD), BF),
            pltpu.VMEM((MEMBERS, PLANES, PAD, PAD), BF),
            pltpu.VMEM((PLANES, MEMBERS, SURFACE), F32),
            pltpu.VMEM(h.shape, BF),
            pltpu.VMEM(second.shape, BF),
            pltpu.VMEM(second_t.shape, BF),
            pltpu.VMEM((RELAY_PLANES, PAD, PAD), BF),
            pltpu.VMEM((RETURN_PLANES, PAD, PAD), BF),
            dma((NQ,)), dma((3,)), dma((NQ,)),
            dma((MEMBERS, NQ)), dma((MEMBERS, NQ)), dma, dma,
            dma((MEMBERS, NQ)), dma((MEMBERS, NQ)), dma((MEMBERS, NQ)),
            dma((MEMBERS, NQ)), dma((MEMBERS, NQ)), dma((MEMBERS, NQ)),
            dma((MEMBERS, NQ)), dma((MEMBERS, NQ)), dma, dma, dma, dma,
        ],
        compiler_params=pltpu.CompilerParams(
            collective_id=0, has_side_effects=True, vmem_limit_bytes=58 * 2**20),
    )(planes_first, occupations, h, second, second_t)
    steps = 5
    total = pl.pallas_call(
        functools.partial(pass_on, steps),
        out_shape=jax.ShapeDtypeStruct(planes_first.shape, F32),
        in_specs=[hbm],
        out_specs=hbm,
        scratch_shapes=[pltpu.VMEM(planes_first.shape, F32), dma((steps,)), dma((steps,))],
        compiler_params=pltpu.CompilerParams(vmem_limit_bytes=58 * 2**20),
    )(total)
    return total.transpose(1, 0, 2)


def solution(mesh):
    return jax.shard_map(
        per_device,
        mesh=mesh,
        in_specs=(P("band", "grid", None), P("band")),
        out_specs=P("band", "grid", None),
        check_vma=False,
    )
```

```python
import functools
import math

import jax
import jax.numpy as jnp
import ml_dtypes
import numpy as np
from jax import lax
from jax.experimental import pallas as pl
from jax.experimental.pallas import tpu as pltpu
from jax.sharding import PartitionSpec as P

COULOMB = 160.0
NG = 120
PAD = 128
GRID = 8
PLANES = 15
MEMBERS = 2
ROWS = 32
TILE = 16
OUT_GROUPS = ((0, 3), (3, 5), (8, 7))
BACK_GROUPS = ((0, 7), (7, 5), (12, 3))
NQ = len(OUT_GROUPS)
EARLY = 2
RELAY_Z = {(0, 1): 3, (0, 2): 2, (1, 1): 4, (1, 2): 1}
HAND_ON = {(0, 2): 0, (1, 1): 1}
RETURN_Z = {0: 6, 1: 5}
RELAY_PLANES = max(OUT_GROUPS[q][1] for _, q in RELAY_Z)
RETURN_PLANES = max(BACK_GROUPS[q][1] for q in RETURN_Z)
SURFACE = NG * NG
MESH = pl.DeviceIdType.MESH
BF = jnp.bfloat16
F32 = jnp.float32


def tables():
    n = np.arange(NG)
    angle = (n[:, None] * n[None, :] % NG).astype(np.float32) * np.float32(2.0 * math.pi / NG)
    h = (np.cos(angle) + np.sin(angle)) / np.float32(math.sqrt(NG))
    padded = np.zeros((PAD, PAD), np.float32)
    padded[:NG, :NG] = h
    second = np.zeros((GRID * ROWS, MEMBERS, PAD), np.float32)
    for p in range(MEMBERS):
        second[p * NG:(p + 1) * NG, p, :NG] = h
    second = second.reshape(GRID * ROWS, MEMBERS * PAD)
    return (
        padded.astype(ml_dtypes.bfloat16),
        second.astype(ml_dtypes.bfloat16),
        np.ascontiguousarray(second.T).astype(ml_dtypes.bfloat16),
    )


def dot(a, b):
    return jnp.dot(a, b, preferred_element_type=F32)


def square(index):
    folded = jnp.where(index <= NG // 2, index, index - NG).astype(F32)
    return folded * folded


def kernel(bands, occ, h_hbm, second_hbm, second_t_hbm, out,
           xin, rows32, own, part, occ_mine, occ_part, coul, send, got, wide, wide2,
           back_send, back, local, ret, ret_got, xout, h_ref, second_ref, second_t_ref, relayed, returned,
           in_sem, c_sem, out_sem, sh_send, sh_recv, oc_send, oc_recv, f_send, f_recv, f_own,
           b_send, b_recv, b_own, r_send, r_recv, re_send, re_recv, rr_send, rr_recv):
    me_b = lax.axis_index("band")
    me = lax.axis_index("grid")
    groups = lax.axis_size("band")
    core = lax.rem(me_b, 2)
    ahead = {"band": lax.rem(me_b + 1, groups)}
    behind = {"band": lax.rem(me_b + groups - 1, groups)}

    side = groups // 2
    column = me_b // side
    place = lax.rem(me_b, side)
    first = place == 0
    last = place == side - 1
    other = (1 - column) * side

    def remote(src, dst, send_sem, recv_sem, to):
        return pltpu.make_async_remote_copy(
            src, dst, send_sem, recv_sem, device_id=to, device_id_type=MESH)

    def out_span(q):
        return pl.ds(*OUT_GROUPS[q])

    def back_span(q):
        return pl.ds(*BACK_GROUPS[q])

    loads = [
        pltpu.make_async_copy(bands.at[out_span(q)], xin.at[out_span(q)], in_sem.at[q]) for q in range(NQ)]
    consts = [
        pltpu.make_async_copy(src, dst, c_sem.at[n])
        for n, (src, dst) in enumerate(
            ((h_hbm, h_ref), (second_hbm, second_ref), (second_t_hbm, second_t_ref)))
    ]
    for c in loads + consts:
        c.start()

    def greet(to):
        pl.semaphore_signal(barrier, inc=1, device_id=to, device_id_type=MESH)

    barrier = pltpu.get_barrier_semaphore()
    for d in range(1, GRID):
        greet({"grid": lax.rem(me + d, GRID)})
    greet(ahead)
    greet(behind)
    greetings = GRID + 1
    for is_source, source, is_target, stops in (
            (last, side - 1, first, [2 * z + 1 for z in RELAY_Z.values()]),
            (first, 0, last, [2 * z for z in RETURN_Z.values()])):
        for stop in stops:
            @pl.when(place == stop)
            def _(source=source):
                greet({"band": other + source})

            @pl.when(is_target)
            def _(stop=stop):
                greet({"band": column * side + stop})
            greetings += (place == stop).astype(jnp.int32)
        greetings += jnp.where(is_source, len(stops), 0)

    lane = lax.broadcasted_iota(jnp.int32, (MEMBERS, PAD), 1)
    rows32[pl.ds(NG * MEMBERS, 8 * MEMBERS), :] = jnp.zeros((8 * MEMBERS, PAD), F32)
    wide[pl.ds(NG * ROWS, 8 * ROWS), :] = jnp.zeros((8 * ROWS, PAD), F32)
    row = lax.broadcasted_iota(jnp.int32, (8, PAD), 0)
    occ_mine[...] = jnp.where(row == 0, occ[0], occ[1])

    def unpack(x, _):
        tiles = {}

        def tile_of(t):
            if t not in tiles:
                if (t + 1) * PAD <= SURFACE:
                    tiles[t] = xin[x, :, t * PAD:(t + 1) * PAD]
                else:
                    half = xin[x, :, t * PAD:SURFACE]
                    tiles[t] = jnp.concatenate([half, jnp.zeros_like(half)], axis=1)
            return tiles[t]

        for r in range(NG):
            tile, off = divmod(NG * r, PAD)
            a = tile_of(tile)
            if off > PAD - NG:
                a = jnp.where(lane >= off, a, tile_of(tile + 1))
            if off:
                a = pltpu.roll(a, PAD - off, 1)
            rows32[pl.ds(r * MEMBERS, MEMBERS), :] = a
        for i in range(MEMBERS):
            own[i, x] = rows32[pl.ds(i, PAD, stride=MEMBERS), :].astype(BF)
        return 0

    shifts = [[
        remote(own.at[j, out_span(q)], part.at[j, out_span(q)], sh_send.at[j, q], sh_recv.at[j, q], ahead)
        for q in range(NQ)] for j in range(MEMBERS)]

    def relay_room(q):
        return relayed.at[pl.ds(0, OUT_GROUPS[q][1])]

    def start_shift(j, q):
        if (j, q) not in RELAY_Z:
            shifts[j][q].start()
            return

        @pl.when(last)
        def _():
            remote(own.at[j, out_span(q)], relay_room(q), sh_send.at[j, q], re_recv,
                   {"band": other + 2 * RELAY_Z[j, q] + 1}).start()

        @pl.when(jnp.logical_not(last))
        def _():
            shifts[j][q].start()

    def handed_on(j, q):
        return remote(relay_room(q), part.at[j, out_span(q)], re_send, sh_recv.at[j, q],
                      {"band": column * side})

    def hand_on(wanted):
        for (j, q), z in RELAY_Z.items():
            if j == wanted:
                @pl.when(place == 2 * z + 1)
                def _(j=j, q=q):
                    remote(relay_room(q), relay_room(q), re_send, re_recv, ahead).wait_recv()
                    handed_on(j, q).start()

    def start_return(j, q):
        if j or q not in RETURN_Z:
            returns[j][q].start()
            return

        @pl.when(first)
        def _():
            remote(ret.at[j, back_span(q)], return_room(q), r_send.at[j, q], rr_recv,
                   {"band": other + 2 * RETURN_Z[q]}).start()

        @pl.when(jnp.logical_not(first))
        def _():
            returns[j][q].start()

    def return_room(q):
        return returned.at[pl.ds(0, BACK_GROUPS[q][1])]

    def handed_back(q):
        return remote(return_room(q), ret_got.at[0, back_span(q)], rr_send, r_recv.at[0, q],
                      {"band": column * side + side - 1})

    def hand_back():
        for q, z in RETURN_Z.items():
            @pl.when(place == 2 * z)
            def _(q=q):
                remote(return_room(q), return_room(q), rr_send, rr_recv, ahead).wait_recv()
                handed_back(q).start()

    occ_shift = remote(occ_mine, occ_part, oc_send, oc_recv, ahead)
    lights = [lax.rem(core + j, 2) * (GRID // 2) + 2 * j + core for j in range(MEMBERS)]

    def row_of(j, g):
        return pl.multiple_of(lax.rem(g + 2 * GRID - 1 - lights[j], GRID) * ROWS, ROWS)

    def by_light(is_light, action):
        pl.when(is_light)(functools.partial(action, TILE))
        pl.when(jnp.logical_not(is_light))(functools.partial(action, ROWS))

    def taken(sem, planes, rows):
        view = send.at[0, pl.ds(0, planes), pl.ds(0, rows)]
        remote(view, view, sem, sem, ahead).wait_recv()

    most, full = (GRID - 2) * ROWS + TILE, (GRID - 1) * ROWS

    def out_sent(j, q):
        @pl.when(me == lights[j])
        def _():
            taken(f_send.at[j, q], OUT_GROUPS[q][1], full)

        @pl.when(me != lights[j])
        def _():
            taken(f_send.at[j, q], OUT_GROUPS[q][1], most)

    def back_sent(j, q):
        by_light(me == lights[j], lambda n: taken(b_send.at[j, q], BACK_GROUPS[q][1], (GRID - 1) * n))

    f_mine = {}

    def advance(j, q):
        shifts[j][q].wait_recv()

        def forward(x, _):
            v = part[j, x]
            d = jnp.concatenate([own[0, x] * v, own[1, x] * v], axis=0)
            t = dot(d, h_ref[...]).astype(BF)
            send[j, x] = dot(second_ref[...], t).astype(BF)
            return 0
        lax.fori_loop(OUT_GROUPS[q][0], sum(OUT_GROUPS[q]), forward, 0, unroll=OUT_GROUPS[q][1])
        if j:
            out_sent(0, q)

        there = pl.ds(me * PLANES + OUT_GROUPS[q][0], OUT_GROUPS[q][1])
        f_mine[j, q] = pltpu.make_async_copy(
            send.at[j, out_span(q), pl.ds(row_of(j, me), ROWS)], got.at[j, there], f_own.at[j, q])
        f_mine[j, q].start()
        for d in range(1, GRID):
            to = lax.rem(me + d, GRID)

            def go(n, to=to):
                remote(send.at[j, out_span(q), pl.ds(row_of(j, to), n)], got.at[j, there, pl.ds(0, n)],
                       f_send.at[j, q], f_recv.at[j, q], {"grid": to}).start()
            by_light(to == lights[j], go)
        if (j, q) in HAND_ON:
            hand_on(HAND_ON[j, q])

    for q in range(NQ):
        loads[q].wait()
        lax.fori_loop(OUT_GROUPS[q][0], sum(OUT_GROUPS[q]), unpack, 0, unroll=OUT_GROUPS[q][1])
        if q == 0:
            pl.semaphore_wait(barrier, greetings)
        start_shift(0, q)
        if q == EARLY:
            for c in consts:
                c.wait()
            advance(0, 0)
    for q in range(NQ):
        start_shift(1, q)
    occ_shift.start()
    for j in range(MEMBERS):
        for q in range(NQ):
            if j or q:
                advance(j, q)

    kx = square(lax.broadcasted_iota(jnp.int32, (PAD, PAD), 0))
    kz = square(lax.broadcasted_iota(jnp.int32, (PAD, PAD), 1))
    plane_sq = kx + kz
    for j in range(MEMBERS):
        start = row_of(j, me)

        def fill(l, _, j=j, start=start):
            s = plane_sq + square(lax.rem(start + l, NG))
            coul[j, l] = jnp.where(s > 0.5, COULOMB / jnp.maximum(s, 1.0), 0.0)
            return 0
        lax.fori_loop(0, ROWS, fill, 0)
    for j in range(MEMBERS):
        back[j, :, pl.ds(MEMBERS * NG, TILE)] = jnp.zeros((PLANES, TILE, PAD), BF)
    for j in range(MEMBERS):
        for q in range(NQ):
            f_mine[j, q].wait()
            by_light(me == lights[j],
                     lambda n, j=j, q=q: taken(f_recv.at[j, q], OUT_GROUPS[q][1], (GRID - 1) * n))

        def widen(x, _, j=j):
            wide[pl.ds(pl.multiple_of(x * ROWS, ROWS), ROWS), :] = got[j, x].astype(F32)
            return 0
        lax.fori_loop(0, NG, widen, 0, unroll=8)

        def solve(l, _, j=j):
            r = jnp.concatenate(
                [wide[pl.ds(l, PAD, stride=ROWS), :], wide[pl.ds(TILE + l, PAD, stride=ROWS), :]], axis=1)
            f = dot(h_ref[...], r.astype(BF))
            f = (f * jnp.concatenate([coul[j, l], coul[j, TILE + l]], axis=1)).astype(BF)
            g = dot(h_ref[...], f)
            wide2[pl.ds(l, PAD, stride=ROWS), :] = g[:, :PAD]
            wide2[pl.ds(TILE + l, PAD, stride=ROWS), :] = g[:, PAD:]
            return 0
        lax.fori_loop(0, TILE, solve, 0, unroll=4)

        for q in range(NQ):
            begin, planes = BACK_GROUPS[q]

            def narrow(g, _, j=j, begin=begin, planes=planes):
                for x in range(planes):
                    at = g * PLANES + begin + x
                    back_send[j, at] = wide2[pl.ds(pl.multiple_of(at * ROWS, ROWS), ROWS), :].astype(BF)
                return 0
            lax.fori_loop(0, GRID, narrow, 0, unroll=2)
            if j:
                back_sent(0, q)

            def go(n, j=j, q=q, begin=begin, planes=planes):
                here = back.at[j, back_span(q), pl.ds(row_of(j, me), n)]
                pltpu.make_async_copy(
                    back_send.at[j, pl.ds(me * PLANES + begin, planes), pl.ds(0, n)], here, b_own.at[j, q]).start()
                for d in range(1, GRID):
                    to = lax.rem(me + d, GRID)
                    remote(back_send.at[j, pl.ds(to * PLANES + begin, planes), pl.ds(0, n)], here,
                           b_send.at[j, q], b_recv.at[j, q], {"grid": to}).start()
            by_light(me == lights[j], go)

    def came_back(j, q):
        begin, planes = BACK_GROUPS[q]

        def wait(n):
            view = back_send.at[j, pl.ds(me * PLANES + begin, planes), pl.ds(0, n)]
            pltpu.make_async_copy(view, back.at[j, back_span(q), pl.ds(row_of(j, me), n)], b_own.at[j, q]).wait()
            taken(b_recv.at[j, q], planes, full if n == TILE else most)
        by_light(me == lights[j], wait)

    occ_shift.wait_recv()
    returns = [[
        remote(ret.at[j, back_span(q)], ret_got.at[j, back_span(q)], r_send.at[j, q], r_recv.at[j, q], behind)
        for q in range(NQ)] for j in range(MEMBERS)]
    for j in range(MEMBERS):
        for q in range(NQ):
            came_back(j, q)

            def inverse(x, _, j=j):
                u = dot(second_t_ref[...], back[j, x]).astype(BF)
                v = dot(u, h_ref[...])
                v0, v1 = v[:PAD], v[PAD:]
                w = part[j, x].astype(F32) * occ_part[pl.ds(j, 1), :]
                if j == 0:
                    local[0, x] = -(v0 * w)
                    local[1, x] = -(v1 * w)
                else:
                    local[0, x] -= v0 * w
                    local[1, x] -= v1 * w
                s = (v0 * (own[0, x].astype(F32) * occ_mine[pl.ds(0, 1), :])
                     + v1 * (own[1, x].astype(F32) * occ_mine[pl.ds(1, 1), :]))
                ret[j, x] = (-s).astype(BF)
                return 0
            lax.fori_loop(BACK_GROUPS[q][0], sum(BACK_GROUPS[q]), inverse, 0, unroll=BACK_GROUPS[q][1])
            start_return(j, q)
            if j and q == 1:
                hand_back()

    def pack(x, _):
        for i in range(MEMBERS):
            rows32[pl.ds(i, PAD, stride=MEMBERS), :] = local[i, x] + ret_got[i, x].astype(F32)
        before = None
        for r in range(NG):
            tile = -(-NG * r // PAD)
            begin = PAD * tile - NG * r
            v = rows32[pl.ds(r * MEMBERS, MEMBERS), :]
            if begin:
                v = pltpu.roll(v, PAD - begin, 1)
            if r % 16:
                t = tile - 1
                z0 = PAD * t - NG * (r - 1)
                xout[x, :, t * PAD:(t + 1) * PAD] = jnp.where(lane < NG - z0, before, v)
            before = v
        xout[x, :, SURFACE - 64:] = before[:, :64]
        return 0

    stores = []
    for q in range(NQ):
        for j in range(MEMBERS):
            returns[j][q].wait_recv()
        lax.fori_loop(BACK_GROUPS[q][0], sum(BACK_GROUPS[q]), pack, 0, unroll=BACK_GROUPS[q][1])
        c = pltpu.make_async_copy(xout.at[back_span(q)], out.at[back_span(q)], out_sem.at[q])
        c.start()
        stores.append(c)

    for c in stores:
        c.wait()
    for c in shifts[0] + shifts[1] + [occ_shift] + returns[0] + returns[1]:
        c.wait_send()
    for (j, q), z in RELAY_Z.items():
        @pl.when(place == 2 * z + 1)
        def _(j=j, q=q):
            handed_on(j, q).wait_send()
    for q, z in RETURN_Z.items():
        @pl.when(place == 2 * z)
        def _(q=q):
            handed_back(q).wait_send()
    for q in range(NQ):
        out_sent(1, q)
        back_sent(1, q)


def pass_on(steps, src, dst, held, in_sem, out_sem):
    planes = PLANES // steps
    spans = [pl.ds(n * planes, planes) for n in range(steps)]
    loads = [pltpu.make_async_copy(src.at[p], held.at[p], in_sem.at[n]) for n, p in enumerate(spans)]
    stores = [pltpu.make_async_copy(held.at[p], dst.at[p], out_sem.at[n]) for n, p in enumerate(spans)]
    for c in loads:
        c.start()
    for load, store in zip(loads, stores):
        load.wait()
        store.start()
    for c in stores:
        c.wait()


def per_device(bands, occupations):
    h, second, second_t = (jnp.asarray(t) for t in tables())
    dma = pltpu.SemaphoreType.DMA
    hbm = pl.BlockSpec(memory_space=pl.ANY)
    planes_first = bands.transpose(1, 0, 2)
    total = pl.pallas_call(
        kernel,
        out_shape=jax.ShapeDtypeStruct(planes_first.shape, F32),
        in_specs=[hbm, pl.BlockSpec(memory_space=pltpu.SMEM), hbm, hbm, hbm],
        out_specs=hbm,
        scratch_shapes=[
            pltpu.VMEM((PLANES, MEMBERS, SURFACE), F32),
            pltpu.VMEM((PAD * MEMBERS, PAD), F32),
            pltpu.VMEM((MEMBERS, PLANES, PAD, PAD), BF),
            pltpu.VMEM((MEMBERS, PLANES, PAD, PAD), BF),
            pltpu.VMEM((8, PAD), F32),
            pltpu.VMEM((8, PAD), F32),
            pltpu.VMEM((MEMBERS, ROWS, PAD, PAD), F32),
            pltpu.VMEM((MEMBERS, PLANES, GRID * ROWS, PAD), BF),
            pltpu.VMEM((MEMBERS, NG, ROWS, PAD), BF),
            pltpu.VMEM((PAD * ROWS, PAD), F32),
            pltpu.VMEM((PAD * ROWS, PAD), F32),
            pltpu.VMEM((MEMBERS, NG, ROWS, PAD), BF),
            pltpu.VMEM((MEMBERS, PLANES, GRID * ROWS, PAD), BF),
            pltpu.VMEM((MEMBERS, PLANES, PAD, PAD), F32),
            pltpu.VMEM((MEMBERS, PLANES, PAD, PAD), BF),
            pltpu.VMEM((MEMBERS, PLANES, PAD, PAD), BF),
            pltpu.VMEM((PLANES, MEMBERS, SURFACE), F32),
            pltpu.VMEM(h.shape, BF),
            pltpu.VMEM(second.shape, BF),
            pltpu.VMEM(second_t.shape, BF),
            pltpu.VMEM((RELAY_PLANES, PAD, PAD), BF),
            pltpu.VMEM((RETURN_PLANES, PAD, PAD), BF),
            dma((NQ,)), dma((3,)), dma((NQ,)),
            dma((MEMBERS, NQ)), dma((MEMBERS, NQ)), dma, dma,
            dma((MEMBERS, NQ)), dma((MEMBERS, NQ)), dma((MEMBERS, NQ)),
            dma((MEMBERS, NQ)), dma((MEMBERS, NQ)), dma((MEMBERS, NQ)),
            dma((MEMBERS, NQ)), dma((MEMBERS, NQ)), dma, dma, dma, dma,
        ],
        compiler_params=pltpu.CompilerParams(
            collective_id=0, has_side_effects=True, vmem_limit_bytes=58 * 2**20),
    )(planes_first, occupations, h, second, second_t)
    steps = 5
    total = pl.pallas_call(
        functools.partial(pass_on, steps),
        out_shape=jax.ShapeDtypeStruct(planes_first.shape, F32),
        in_specs=[hbm],
        out_specs=hbm,
        scratch_shapes=[pltpu.VMEM(planes_first.shape, F32), dma((steps,)), dma((steps,))],
        compiler_params=pltpu.CompilerParams(vmem_limit_bytes=58 * 2**20),
    )(total)
    return total.transpose(1, 0, 2)


def solution(mesh):
    return jax.shard_map(
        per_device,
        mesh=mesh,
        in_specs=(P("band", "grid", None), P("band")),
        out_specs=P("band", "grid", None),
        check_vma=False,
    )
```
